256 devices in a mesh: video: 8 (over x, core), tm: 32 (over z, y).
Axes of the slice: x: 4, y: 4, z: 8, core: 2. Of those that a mesh axis runs over, the one named last changes fastest.
Arguments:
- queries: bfloat16 [8, 32, 4096, 256], P('video', 'tm'), may hold values from -720 to 720
- memory: bfloat16 [8, 32, 64, 4096], P('video', 'tm'), may hold values from -6 to 6
- tpos: float32 [7, 64], replicated, may hold values from -4 to 4
- w_k: bfloat16 [64, 256], replicated, may hold values from -0.75 to 0.75
- w_v: bfloat16 [64, 256], replicated, may hold values from -0.75 to 0.75
- w_o: bfloat16 [256, 256], replicated, may hold values from -0.375 to 0.375
- keyframes: int32 [8, 32, 64], P('video', 'tm'), may hold values from 0 to 2047, as said below
- cot: bfloat16 [8, 32, 4096, 256], P('video', 'tm'), may hold values from -6 to 6
Outputs:
- branch: bfloat16 [8, 32, 4096, 256], P('video', 'tm')
- grad_wo: float32 [256, 256], P('tm')
The draws below stay inside these ranges and needn't reach their ends.
Inputs may be any that keep to these rules, and one draw needn't show every extreme that they name: `keyframes`: each frame's list is made of runs of 4 consecutive entries that lie in one frame; the runs of one list lie in different frames.
All inputs are finite; a program needn't handle non-finite values.
Results may differ from the reference program's by a relative error of at most 0.012.
The reference program's roundings to bfloat16 on the way count: a program that leaves them out, or rounds other values in their place, can miss the bound.
Values may be sent and summed in bfloat16 or wider, within the bound.
No kernel may reach another device: no remote copies, remote signals or barrier semaphores. Data moves between devices by JAX's collectives and lax.ppermute only.
A program may use at most 128 MiB of HBM per device.

```python
import math
import jax
import jax.numpy as jnp
from jax import lax

D = 256
MD = 64
TT = 64
TILES = 64
KF = 64
KSEL = 8
CLASSES = 8
TPF = 4096
FRAMES = 32
VIDEOS = 8
CAP = 4


def draw_queries(key, part):
    shape = (VIDEOS, FRAMES, TPF, D)
    values = 1.5 * jax.random.normal(key, shape, jnp.float32)
    return jnp.clip(values, -9.0, 9.0).astype(jnp.bfloat16)


def draw_keyframes(key, part):
    groups = KF // CAP
    key_hot, key_score, key_tile = jax.random.split(key, 3)
    hot_count = max(1, FRAMES // 8)
    hot_keys = jax.random.split(key_hot, VIDEOS)
    orders = jnp.stack([jax.random.permutation(hot_keys[video_idx], FRAMES) for video_idx in range(VIDEOS)])
    owner_ids = jnp.arange(FRAMES, dtype=jnp.int32)
    hot_flag = jnp.any(owner_ids[None, :, None] == orders[:, None, :hot_count], axis=-1).astype(jnp.int32)
    scores = jax.random.randint(key_score, (VIDEOS, FRAMES, FRAMES), 0, 1024, dtype=jnp.int32)
    scores = scores + 768 * hot_flag[:, None, :]
    distinct = scores * FRAMES + owner_ids[None, None, :]
    chosen = lax.top_k(distinct, groups)[1].astype(jnp.int32)
    owners = jnp.repeat(chosen, CAP, axis=-1)
    tile_pick = jax.random.randint(key_tile, (VIDEOS, FRAMES, KF), 0, TILES, dtype=jnp.int32)
    return (owners * TILES + tile_pick).astype(jnp.int32)


def steps_of(stream_key, extent, cuts, least, largest):
    factor_of = 1.0
    for dim, blocks in cuts:
        draws = jax.random.uniform(jax.random.fold_in(jax.random.fold_in(stream_key, 6), dim), (blocks,), jnp.float32, least / len(cuts), largest / len(cuts))
        factor_of = factor_of * jnp.repeat(jnp.exp(draws), extent[dim] // blocks).reshape((-1,) + (1,) * (len(extent) - 1 - dim))
    return factor_of


def bell_draw(own_key, shape, deviation, limit, cuts=(), held_as=jnp.bfloat16):
    entries = deviation * jax.random.normal(own_key, shape, jnp.float32)
    if cuts:
        entries = entries * steps_of(own_key, shape, cuts, -0.22, 0.18)
    return jnp.clip(entries, -limit, limit).astype(held_as)


def setup_inputs(seed: int = 0) -> dict:
    streams_of = jax.random.split(jax.random.key(seed), 9)
    queries = draw_queries(jax.random.fold_in(streams_of[8], 71), 0)
    memory = bell_draw(streams_of[1], (VIDEOS, FRAMES, TILES, TT * MD), 1.0, 6.0, ((0, 8), (1, 32)))
    tpos = bell_draw(streams_of[2], (7, MD), 1.0, 4.0, (), jnp.float32)
    w_k = bell_draw(streams_of[3], (MD, D), MD ** -0.5, 0.75)
    w_v = bell_draw(streams_of[4], (MD, D), MD ** -0.5, 0.75)
    w_o = bell_draw(streams_of[5], (D, D), D ** -0.5, 0.375)
    keyframes = draw_keyframes(jax.random.fold_in(streams_of[8], 71), 0)
    cot = bell_draw(streams_of[7], (VIDEOS, FRAMES, TPF, D), 1.0, 6.0, ((0, 8), (1, 32)))
    return dict(queries=queries, memory=memory, tpos=tpos, w_k=w_k, w_v=w_v, w_o=w_o, keyframes=keyframes, cot=cot)


def project_pairs(tiles, position, w_pair):
    leading = tiles.shape[:-1]
    mixed = tiles.reshape(leading + (TT, MD)).astype(jnp.float32) + position
    mixed = mixed.astype(jnp.bfloat16)
    kv_pairs = jnp.dot(mixed.reshape(-1, MD), w_pair, preferred_element_type=jnp.float32)
    return kv_pairs.astype(jnp.bfloat16).reshape(leading + (TT, 2 * D))

def attend(query_tiles, recent_pairs, keyed_pairs, valid_back):
    tile_num = query_tiles.shape[0]
    recent = jnp.transpose(recent_pairs, (1, 0, 2, 3))
    kv_pairs = jnp.concatenate([recent, keyed_pairs], axis=1).reshape(tile_num, (6 + KSEL) * TT, 2 * D)
    key_part = kv_pairs[..., :D]
    value_part = kv_pairs[..., D:]
    scores = jnp.einsum('tqd,tkd->tqk', query_tiles.astype(jnp.float32), key_part.astype(jnp.float32))
    scores = scores * (1.0 / math.sqrt(D))
    live_keys = jnp.concatenate([jnp.repeat(valid_back, TT), jnp.ones((KSEL * TT,), dtype=bool)])
    scores = jnp.where(live_keys[None, None, :], scores, -jnp.inf)
    row_max = lax.optimization_barrier(jnp.max(scores, axis=-1, keepdims=True))
    weights = jnp.exp(scores - row_max)
    weights = (weights / lax.optimization_barrier(jnp.sum(weights, axis=-1, keepdims=True))).astype(jnp.bfloat16)
    attended = jnp.einsum('tqk,tkd->tqd', weights.astype(jnp.float32), value_part.astype(jnp.float32))
    return attended.astype(jnp.bfloat16)

def reference(queries, memory, tpos, w_k, w_v, w_o, keyframes, cot):
    w_pair = jnp.concatenate([w_k, w_v], axis=1)
    offsets = jnp.arange(1, 7, dtype=jnp.int32)
    tile_ids = jnp.arange(TILES, dtype=jnp.int32)
    entry_ids = (tile_ids % CLASSES)[:, None] + CLASSES * jnp.arange(KSEL, dtype=jnp.int32)[None, :]

    def one_frame(frame_index):
        video_idx = frame_index // FRAMES
        frame_idx = frame_index % FRAMES
        frames = memory[video_idx]
        back_frame = frame_idx - offsets
        valid_back = back_frame >= 0
        recent_raw = frames[jnp.maximum(back_frame, 0)]
        recent_pairs = project_pairs(recent_raw, tpos[:6][:, None, None, :], w_pair)
        keyed_raw = frames.reshape(FRAMES * TILES, TT * MD)[keyframes[video_idx, frame_idx]]
        keyed_all = project_pairs(keyed_raw, tpos[6], w_pair)
        keyed_pairs = keyed_all[entry_ids]
        query_tiles = queries[video_idx, frame_idx].reshape(TILES, TT, D)
        return attend(query_tiles, recent_pairs, keyed_pairs, valid_back).reshape(TPF, D)
    attended = lax.map(one_frame, jnp.arange(VIDEOS * FRAMES, dtype=jnp.int32))
    flat = attended.reshape(-1, D)
    branch = jnp.dot(flat, w_o, preferred_element_type=jnp.float32).astype(jnp.bfloat16)
    grad_wo = jnp.dot(flat.T, cot.reshape(-1, D), preferred_element_type=jnp.float32)
    grad_wo = grad_wo / math.sqrt(VIDEOS * FRAMES * TPF)
    return (branch.reshape(queries.shape), grad_wo)
```

```python
import math

import jax
import jax.numpy as jnp
from jax import lax
from jax.experimental import pallas as pl
from jax.experimental.pallas import tpu as pltpu
from jax.sharding import PartitionSpec as P

D = 256
MD = 64
TT = 64
TILES = 64
KF = 64
KSEL = 8
CLASSES = 8
RUN = 4
RING = 4
PAIRS = TT // 2
LANES = 2 * MD
BLOCK = 8
LOW = -1e30
EXP2_SCALE = math.log2(math.e) / math.sqrt(D)
MIB = 1024 * 1024


def routed(shard, rows, target):
    pairs = []
    for row in range(rows):
        for place in range(RING):
            to = target(row, place)
            if to is not None and to[0] < rows:
                pairs.append((row * RING + place, to[0] * RING + to[1]))
    return lax.ppermute(shard, "tm", pairs)


def project(tiles, position, w_pair):
    mixed = (tiles.astype(jnp.float32) + position).astype(jnp.bfloat16)
    pairs = jnp.dot(mixed.reshape(-1, LANES), w_pair, preferred_element_type=jnp.float32)
    return pairs.astype(jnp.bfloat16)


def pick_kernel(asked, own, outgoing):
    def one(dest, carry):
        for slot in range(RUN):
            outgoing[dest * RUN + slot] = own[asked[dest, slot]]
        return carry

    lax.fori_loop(0, asked.shape[0], one, 0)


def recent_kernel(place, q, b1, c1, b2, c3, b3, c2, a, d2, d1, z2, tpos, w_pair, acc, stat, keys, values):
    frame = place[0]
    y = frame % RING
    f32 = lambda ref: ref[...].astype(jnp.float32)
    picked = (
        lambda: jnp.where(y == 0, f32(c1), f32(b1)),
        lambda: jnp.where(y < 2, f32(c3), f32(b2)),
        lambda: jnp.where(y == 3, f32(b3), f32(c2)),
        lambda: f32(a),
        lambda: jnp.where(y == 0, f32(d2), f32(c1)),
        lambda: jnp.where(y < 2, f32(d1), f32(z2)),
    )
    for j in range(6):
        pairs = project(picked[j](), tpos[j : j + 1, :], w_pair[...])
        for part, ref in enumerate((keys, values)):
            for odd in range(2):
                first = (2 * part + odd) * D
                ref[:, odd * 6 + j] = pairs[:, first : first + D].reshape(BLOCK, PAIRS, D)
    column = lax.broadcasted_iota(jnp.int32, (1, 6 * TT), 1)
    offset = (column % (6 * PAIRS)) // PAIRS + 1
    bias = jnp.where(offset <= frame, 0.0, LOW).astype(jnp.float32)
    for t in range(BLOCK):
        scores = lax.dot_general(
            q[t], keys[t].reshape(6 * TT, D), (((1,), (1,)), ((), ())), preferred_element_type=jnp.float32
        )
        scores = scores * EXP2_SCALE + bias
        top = jnp.max(scores, axis=-1, keepdims=True)
        weights = jnp.exp2(scores - top)
        stat[t, :, 0:1] = top
        stat[t, :, 1:2] = jnp.sum(weights, axis=-1, keepdims=True)
        acc[t] = jnp.dot(
            weights.astype(jnp.bfloat16), values[t].reshape(6 * TT, D), preferred_element_type=jnp.float32
        )


def keyed_kernel(owners, q, incoming, tpos, w_pair, acc, stat, w_o, cot, branch, grad, tiles):
    c = pl.program_id(0)
    for s in range(KSEL):
        tiles[s] = incoming[owners[2 * s + c // RUN] * RUN + c % RUN]
    pairs = project(tiles[...], tpos[6:7, :], w_pair[...])
    keys = jnp.concatenate([pairs[:, :D], pairs[:, D : 2 * D]], axis=0)
    values = jnp.concatenate([pairs[:, 2 * D : 3 * D], pairs[:, 3 * D :]], axis=0)
    rows = q.shape[0] * TT
    scores = lax.dot_general(
        q[...].reshape(rows, D), keys, (((1,), (1,)), ((), ())), preferred_element_type=jnp.float32
    )
    scores = scores * EXP2_SCALE
    top_near = stat[...].reshape(rows, 2)[:, 0:1]
    sum_near = stat[...].reshape(rows, 2)[:, 1:2]
    top = jnp.maximum(jnp.max(scores, axis=-1, keepdims=True), top_near)
    weights = jnp.exp2(scores - top)
    near = jnp.exp2(top_near - top)
    total = jnp.sum(weights, axis=-1, keepdims=True) + sum_near * near
    summed = jnp.dot(weights.astype(jnp.bfloat16), values, preferred_element_type=jnp.float32)
    summed = (summed + acc[...].reshape(rows, D) * near) / total
    attended = summed.astype(jnp.bfloat16)
    out = jnp.dot(attended, w_o[...], preferred_element_type=jnp.float32).astype(jnp.bfloat16)
    branch[...] = out.reshape(branch.shape)
    term = lax.dot_general(
        attended, cot[...].reshape(rows, D), (((0,), (0,)), ((), ())), preferred_element_type=jnp.float32
    )

    @pl.when(c == 0)
    def _():
        grad[...] = term

    @pl.when(c > 0)
    def _():
        grad[...] += term


def per_device(queries, memory, tpos, w_k, w_v, w_o, keyframes, cot):
    device_index = lax.axis_index("tm")
    devices = lax.axis_size("tm")
    rows = devices // RING
    groups = TILES // CLASSES
    own = memory[0, 0].reshape(TILES, PAIRS, LANES)

    run_ids = keyframes[0, 0].reshape(KF // RUN, RUN)
    owners = run_ids[:, 0] // TILES
    hits = owners[None, :, None] == jnp.arange(devices, dtype=jnp.int32)[:, None, None]
    asks = jnp.sum(jnp.where(hits, run_ids[None] % TILES, 0), axis=1)
    asked = lax.all_to_all(asks, "tm", split_axis=0, concat_axis=0, tiled=True)

    a = routed(own, rows, lambda z, y: (z + 1, y))
    b1 = routed(own, rows, lambda z, y: (z, y + 1) if y < 3 else None)
    b2 = routed(own, rows, lambda z, y: (z, y + 2) if y < 2 else None)
    b3 = routed(own, rows, lambda z, y: (z, 3) if y == 0 else None)
    c1 = routed(a, rows, lambda z, y: (z, (y + 1) % RING))
    c2 = routed(a, rows, lambda z, y: (z, y - 1) if y > 0 else None)
    c3 = routed(a, rows, lambda z, y: (z, y - 2) if y > 1 else None)
    z2 = routed(b2, rows, lambda z, y: (z + 1, y) if y > 1 else None)
    d1 = routed(c3, rows, lambda z, y: (z + 1, y) if y < 2 else None)
    d2 = routed(c1, rows, lambda z, y: (z + 1, y) if y == 0 else None)

    outgoing = pl.pallas_call(
        pick_kernel,
        out_shape=jax.ShapeDtypeStruct((devices * RUN, PAIRS, LANES), jnp.bfloat16),
        in_specs=[pl.BlockSpec(memory_space=pltpu.SMEM), pl.BlockSpec(memory_space=pltpu.VMEM)],
        out_specs=pl.BlockSpec(memory_space=pltpu.VMEM),
        compiler_params=pltpu.CompilerParams(vmem_limit_bytes=8 * MIB),
        name="pick",
    )(asked, own)
    incoming = lax.all_to_all(outgoing, "tm", split_axis=0, concat_axis=0, tiled=True)

    zero = jnp.zeros_like(w_k)
    w_pair = jnp.concatenate(
        [
            jnp.concatenate([w_k, zero, w_v, zero], axis=1),
            jnp.concatenate([zero, w_k, zero, w_v], axis=1),
        ],
        axis=0,
    )
    tpos_pair = jnp.concatenate([tpos, tpos], axis=1)
    q_tiles = queries[0, 0].reshape(TILES, TT, D)
    whole = lambda *shape: pl.BlockSpec(shape, lambda i, *_: (0,) * len(shape))
    tile_block = pl.BlockSpec((BLOCK, PAIRS, LANES), lambda i, *_: (i, 0, 0))
    row_block = pl.BlockSpec((BLOCK, TT, D), lambda i, *_: (i, 0, 0))
    acc, stat = pl.pallas_call(
        recent_kernel,
        grid_spec=pltpu.PrefetchScalarGridSpec(
            num_scalar_prefetch=1,
            grid=(TILES // BLOCK,),
            in_specs=[row_block] + [tile_block] * 10 + [whole(7, LANES), whole(LANES, 4 * D)],
            out_specs=[row_block, pl.BlockSpec((BLOCK, TT, 2), lambda i, *_: (i, 0, 0))],
            scratch_shapes=[pltpu.VMEM((BLOCK, 12, PAIRS, D), jnp.bfloat16)] * 2,
        ),
        out_shape=[
            jax.ShapeDtypeStruct((TILES, TT, D), jnp.float32),
            jax.ShapeDtypeStruct((TILES, TT, 2), jnp.float32),
        ],
        compiler_params=pltpu.CompilerParams(vmem_limit_bytes=40 * MIB),
        name="recent",
    )(device_index[None], q_tiles, b1, c1, b2, c3, b3, c2, a, d2, d1, z2, tpos_pair, w_pair)

    by_class = lambda x: x.reshape((groups, CLASSES) + x.shape[1:])
    class_block = lambda width: pl.BlockSpec((groups, 1, TT, width), lambda i, *_: (0, i, 0, 0))
    branch, grad = pl.pallas_call(
        keyed_kernel,
        grid_spec=pltpu.PrefetchScalarGridSpec(
            num_scalar_prefetch=1,
            grid=(CLASSES,),
            in_specs=[
                class_block(D),
                whole(devices * RUN, PAIRS, LANES),
                whole(7, LANES),
                whole(LANES, 4 * D),
                class_block(D),
                class_block(2),
                whole(D, D),
                class_block(D),
            ],
            out_specs=[class_block(D), whole(D, D)],
            scratch_shapes=[pltpu.VMEM((KSEL, PAIRS, LANES), jnp.bfloat16)],
        ),
        out_shape=[
            jax.ShapeDtypeStruct((groups, CLASSES, TT, D), jnp.bfloat16),
            jax.ShapeDtypeStruct((D, D), jnp.float32),
        ],
        compiler_params=pltpu.CompilerParams(vmem_limit_bytes=40 * MIB),
        name="keyed",
    )(
        owners,
        by_class(q_tiles),
        incoming,
        tpos_pair,
        w_pair,
        by_class(acc),
        by_class(stat),
        w_o,
        by_class(cot[0, 0].reshape(TILES, TT, D)),
    )

    parts = lax.all_to_all(
        grad.reshape(devices, D // devices, D), "tm", split_axis=0, concat_axis=0, tiled=True
    )
    videos = lax.axis_size("video")
    summed = jnp.sum(parts, axis=0) * (1.0 / math.sqrt(videos * devices * TILES * TT))
    step = 1
    while step < videos:
        summed = summed + lax.ppermute(summed, "video", [(i, i ^ step) for i in range(videos)])
        step *= 2
    return branch.reshape(queries.shape), summed


def solution(mesh):
    in_specs = (
        P("video", "tm", None, None),
        P("video", "tm", None, None),
        P(),
        P(),
        P(),
        P(),
        P("video", "tm", None),
        P("video", "tm", None, None),
    )
    out_specs = (P("video", "tm", None, None), P("tm", None))
    return jax.shard_map(
        per_device, mesh=mesh, in_specs=in_specs, out_specs=out_specs, check_vma=False
    )
```

```python
import math

import jax
import jax.numpy as jnp
from jax import lax
from jax.experimental import pallas as pl
from jax.experimental.pallas import tpu as pltpu
from jax.sharding import PartitionSpec as P

D = 256
MD = 64
TT = 64
TILES = 64
KF = 64
KSEL = 8
CLASSES = 8
RUN = 4
RING = 4
PAIRS = TT // 2
LANES = 2 * MD
BLOCK = 16
NEAR = 4
LOW = -1e30
EXP2_SCALE = math.log2(math.e) / math.sqrt(D)
MIB = 1024 * 1024


def routed(shard, rows, target):
    pairs = []
    for row in range(rows):
        for place in range(RING):
            to = target(row, place)
            if to is not None and to[0] < rows:
                pairs.append((row * RING + place, to[0] * RING + to[1]))
    return lax.ppermute(shard, "tm", pairs)


def mix(tiles, position):
    return (tiles.astype(jnp.float32) + position).astype(jnp.bfloat16)


def times(left, right):
    return jnp.dot(left, right, preferred_element_type=jnp.float32)


def against(queries, pairs):
    keys = jnp.concatenate([pairs[:, :D], pairs[:, D:]], axis=0)
    return lax.dot_general(queries, keys, (((1,), (1,)), ((), ())), preferred_element_type=jnp.float32)


def gathered(weights, mixed):
    rows, pairs = weights.shape[0], mixed.shape[0]
    both = times(jnp.concatenate([weights[:, :pairs], weights[:, pairs:]], axis=0), mixed)
    lane = lax.broadcasted_iota(jnp.int32, (rows, LANES), 1)
    return jnp.where(lane < MD, both[:rows], both[rows:])


def absent(frame, first, count):
    column = lax.broadcasted_iota(jnp.int32, (1, 2 * count * PAIRS), 1)
    offset = (column // PAIRS) % count + first
    return jnp.where(offset <= frame, 0.0, LOW).astype(jnp.float32)


def ask_kernel(listed, asks):
    shape = asks.shape
    dest = lax.broadcasted_iota(jnp.int32, shape, 0)
    lane = lax.broadcasted_iota(jnp.int32, shape, 1)
    total = jnp.zeros(shape, jnp.int32)
    for run in range(KF // RUN):
        owner = listed[run * RUN] // TILES
        for slot in range(RUN):
            hit = (dest == owner) & (lane == slot)
            total = jnp.where(hit, listed[run * RUN + slot] % TILES, total)
    asks[...] = total


def pick_kernel(asked, own, *rest):
    outgoing = rest[-1]

    def one(dest, carry):
        for slot in range(RUN):
            outgoing[dest * RUN + slot] = own[asked[dest, slot]]
        return carry

    lax.fori_loop(0, asked.shape[0], one, 0)


def near_kernel(place, q, b1, c1, b2, c3, b3, c2, a, tpos, w_key, near, mixed):
    frame = place[0]
    y = frame % RING
    mixed[:, 0] = mix(jnp.where(y == 0, c1[...], b1[...]), tpos[0:1, :])
    mixed[:, 1] = mix(jnp.where(y < 2, c3[...], b2[...]), tpos[1:2, :])
    mixed[:, 2] = mix(jnp.where(y == 3, b3[...], c2[...]), tpos[2:3, :])
    mixed[:, 3] = mix(a[...], tpos[3:4, :])
    rows = NEAR * PAIRS
    flat = mixed[...].reshape(BLOCK * rows, LANES)
    pairs = times(flat, w_key[...]).astype(jnp.bfloat16)
    tiles = range(BLOCK)
    scores = jnp.concatenate([against(q[t], pairs[t * rows : (t + 1) * rows]) for t in tiles], axis=0)
    scores = scores * EXP2_SCALE + absent(frame, 1, NEAR)
    top = jnp.max(scores, axis=-1, keepdims=True)
    weights = jnp.exp2(scores - top)
    total = jnp.sum(weights, axis=-1, keepdims=True)
    weights = weights.astype(jnp.bfloat16)
    summed = jnp.concatenate(
        [gathered(weights[t * TT : (t + 1) * TT], flat[t * rows : (t + 1) * rows]) for t in tiles], axis=0
    )
    summed = summed + pltpu.roll(summed, MD, 1)
    lane = lax.broadcasted_iota(jnp.int32, summed.shape, 1)
    packed = jnp.where(lane < MD, summed, jnp.where(lane < MD + PAIRS, top, total))
    near[...] = packed.reshape(near.shape)


def final_kernel(
    place, listed, q, incoming, c1, d2, d1, z2, near, tpos, w_key, w_value, w_o, cot, branch, grad, tiles, mixed
):
    frame = place[0]
    y = frame % RING
    c = pl.program_id(0)
    for s in range(KSEL):
        run = 2 * s + c // RUN
        tiles[s] = incoming[(listed[run * RUN] // TILES) * RUN + c % RUN]
    keyed = mix(tiles[...], tpos[6:7, :]).reshape(KSEL * PAIRS, LANES)
    keyed_pairs = times(keyed, w_key[...]).astype(jnp.bfloat16)
    mixed[:, 0] = mix(jnp.where(y == 0, d2[:, 0], c1[:, 0]), tpos[4:5, :])
    mixed[:, 1] = mix(jnp.where(y < 2, d1[:, 0], z2[:, 0]), tpos[5:6, :])
    far_rows = 2 * PAIRS
    count = q.shape[0]
    rows = count * TT
    far = mixed[...].reshape(count * far_rows, LANES)
    far_pairs = times(far, w_key[...]).astype(jnp.bfloat16)
    queries = q[...].reshape(rows, D)
    scores = against(queries, keyed_pairs) * EXP2_SCALE
    far_scores = jnp.concatenate(
        [against(q[t, 0], far_pairs[t * far_rows : (t + 1) * far_rows]) for t in range(count)], axis=0
    )
    far_scores = far_scores * EXP2_SCALE + absent(frame, NEAR + 1, 2)
    packed = near[...].reshape(rows, LANES)
    near_top = packed[:, MD : MD + 1]
    near_sum = packed[:, MD + PAIRS : MD + PAIRS + 1]
    top = jnp.maximum(jnp.max(scores, axis=-1, keepdims=True), jnp.max(far_scores, axis=-1, keepdims=True))
    top = jnp.maximum(top, near_top)
    weights = jnp.exp2(scores - top)
    far_weights = jnp.exp2(far_scores - top)
    near_scale = jnp.exp2(near_top - top)
    total = jnp.sum(weights, axis=-1, keepdims=True) + jnp.sum(far_weights, axis=-1, keepdims=True)
    total = total + near_sum * near_scale
    weights = weights.astype(jnp.bfloat16)
    far_weights = far_weights.astype(jnp.bfloat16)
    summed = gathered(weights, keyed) + jnp.concatenate(
        [
            gathered(far_weights[t * TT : (t + 1) * TT], far[t * far_rows : (t + 1) * far_rows])
            for t in range(count)
        ],
        axis=0,
    )
    lane = lax.broadcasted_iota(jnp.int32, (rows, LANES), 1)
    summed = (summed + jnp.where(lane < MD, packed, 0.0) * near_scale) / total
    high = summed.astype(jnp.bfloat16)
    low = (summed - high.astype(jnp.float32)).astype(jnp.bfloat16)
    attended = times(jnp.concatenate([high, low], axis=1), w_value[...]).astype(jnp.bfloat16)
    branch[...] = times(attended, w_o[...]).astype(jnp.bfloat16).reshape(branch.shape)
    term = lax.dot_general(
        attended, cot[...].reshape(rows, D), (((0,), (0,)), ((), ())), preferred_element_type=jnp.float32
    )

    @pl.when(c == 0)
    def _():
        grad[...] = term

    @pl.when(c > 0)
    def _():
        grad[...] += term


def per_device(queries, memory, tpos, w_k, w_v, w_o, keyframes, cot):
    place = lax.axis_index("tm")[None]
    devices = lax.axis_size("tm")
    rows = devices // RING
    groups = TILES // CLASSES
    own = memory[0, 0].reshape(TILES, PAIRS, LANES)
    listed = keyframes.reshape(KF)
    in_smem = pl.BlockSpec(memory_space=pltpu.SMEM)
    in_vmem = pl.BlockSpec(memory_space=pltpu.VMEM)

    asks = pl.pallas_call(
        ask_kernel,
        out_shape=jax.ShapeDtypeStruct((devices, LANES), jnp.int32),
        in_specs=[in_smem],
        out_specs=in_vmem,
        name="ask",
    )(listed)
    a = routed(own, rows, lambda z, y: (z + 1, y))
    b1 = routed(own, rows, lambda z, y: (z, y + 1) if y < 3 else None)
    b2 = routed(own, rows, lambda z, y: (z, y + 2) if y < 2 else None)
    b3 = routed(own, rows, lambda z, y: (z, 3) if y == 0 else None)
    asked = lax.all_to_all(asks, "tm", split_axis=0, concat_axis=0, tiled=True)
    outgoing = pl.pallas_call(
        pick_kernel,
        out_shape=jax.ShapeDtypeStruct((devices * RUN, PAIRS, LANES), jnp.bfloat16),
        in_specs=[in_smem, in_vmem] + [pl.BlockSpec(memory_space=pl.ANY)] * 3,
        out_specs=in_vmem,
        compiler_params=pltpu.CompilerParams(vmem_limit_bytes=56 * MIB),
        name="pick",
    )(asked, own, a, b1, b3)
    incoming = lax.all_to_all(outgoing, "tm", split_axis=0, concat_axis=0, tiled=True)
    c1 = routed(a, rows, lambda z, y: (z, (y + 1) % RING))
    c2 = routed(a, rows, lambda z, y: (z, y - 1) if y > 0 else None)
    c3 = routed(a, rows, lambda z, y: (z, y - 2) if y > 1 else None)
    z2 = routed(b2, rows, lambda z, y: (z + 1, y) if y > 1 else None)
    d1 = routed(c3, rows, lambda z, y: (z + 1, y) if y < 2 else None)
    d2 = routed(c1, rows, lambda z, y: (z + 1, y) if y == 0 else None)

    zero = jnp.zeros_like(w_k)
    w_key = jnp.concatenate(
        [jnp.concatenate([w_k, zero], axis=1), jnp.concatenate([zero, w_k], axis=1)], axis=0
    )
    w_value = jnp.concatenate([w_v] * 4, axis=0)
    tpos_pair = jnp.concatenate([tpos, tpos], axis=1)
    q_tiles = queries[0, 0].reshape(TILES, TT, D)
    whole = lambda *shape: pl.BlockSpec(shape, lambda i, *_: (0,) * len(shape))
    tile_block = pl.BlockSpec((BLOCK, PAIRS, LANES), lambda i, *_: (i, 0, 0))
    row_block = lambda width: pl.BlockSpec((BLOCK, TT, width), lambda i, *_: (i, 0, 0))
    near = pl.pallas_call(
        near_kernel,
        grid_spec=pltpu.PrefetchScalarGridSpec(
            num_scalar_prefetch=1,
            grid=(TILES // BLOCK,),
            in_specs=[row_block(D)] + [tile_block] * 7 + [whole(7, LANES), whole(LANES, 2 * D)],
            out_specs=row_block(LANES),
            scratch_shapes=[pltpu.VMEM((BLOCK, NEAR, PAIRS, LANES), jnp.bfloat16)],
        ),
        out_shape=jax.ShapeDtypeStruct((TILES, TT, LANES), jnp.float32),
        compiler_params=pltpu.CompilerParams(vmem_limit_bytes=56 * MIB),
        name="near",
    )(place, q_tiles, b1, c1, b2, c3, b3, c2, a, tpos_pair, w_key)

    by_class = lambda x: x.reshape((groups, CLASSES) + x.shape[1:])
    class_block = lambda *tile: pl.BlockSpec((groups, 1) + tile, lambda i, *_: (0, i) + (0,) * len(tile))
    branch, grad = pl.pallas_call(
        final_kernel,
        grid_spec=pltpu.PrefetchScalarGridSpec(
            num_scalar_prefetch=2,
            grid=(CLASSES,),
            in_specs=[class_block(TT, D), whole(devices * RUN, PAIRS, LANES)]
            + [class_block(PAIRS, LANES)] * 4
            + [
                class_block(TT, LANES),
                whole(7, LANES),
                whole(LANES, 2 * D),
                whole(2 * LANES, D),
                whole(D, D),
                class_block(TT, D),
            ],
            out_specs=[class_block(TT, D), whole(D, D)],
            scratch_shapes=[
                pltpu.VMEM((KSEL, PAIRS, LANES), jnp.bfloat16),
                pltpu.VMEM((groups, 2, PAIRS, LANES), jnp.bfloat16),
            ],
        ),
        out_shape=[
            jax.ShapeDtypeStruct((groups, CLASSES, TT, D), jnp.bfloat16),
            jax.ShapeDtypeStruct((D, D), jnp.float32),
        ],
        compiler_params=pltpu.CompilerParams(vmem_limit_bytes=56 * MIB),
        name="final",
    )(
        place,
        listed,
        by_class(q_tiles),
        incoming,
        by_class(c1),
        by_class(d2),
        by_class(d1),
        by_class(z2),
        by_class(near),
        tpos_pair,
        w_key,
        w_value,
        w_o,
        by_class(cot[0, 0].reshape(TILES, TT, D)),
    )

    parts = lax.all_to_all(
        grad.reshape(devices, D // devices, D), "tm", split_axis=0, concat_axis=0, tiled=True
    )
    videos = lax.axis_size("video")
    summed = jnp.sum(parts, axis=0) * (1.0 / math.sqrt(videos * devices * TILES * TT))
    step = 1
    while step < videos:
        summed = summed + lax.ppermute(summed, "video", [(i, i ^ step) for i in range(videos)])
        step *= 2
    return branch.reshape(queries.shape), summed


def solution(mesh):
    in_specs = (
        P("video", "tm", None, None),
        P("video", "tm", None, None),
        P(),
        P(),
        P(),
        P(),
        P("video", "tm", None),
        P("video", "tm", None, None),
    )
    out_specs = (P("video", "tm", None, None), P("tm", None))
    return jax.shard_map(
        per_device, mesh=mesh, in_specs=in_specs, out_specs=out_specs, check_vma=False
    )
```

```python
import math

import jax
import jax.numpy as jnp
from jax import lax
from jax.experimental import pallas as pl
from jax.experimental.pallas import tpu as pltpu
from jax.sharding import PartitionSpec as P

D = 256
MD = 64
TT = 64
TILES = 64
KF = 64
KSEL = 8
CLASSES = 8
RUN = 4
RING = 4
PAIRS = TT // 2
LANES = 2 * MD
BLOCK = 16
EARLY = (1, 4)
LATE = (2, 3, 5, 6)
SHARED = 4
LOW = -1e30
EXP2_SCALE = math.log2(math.e) / math.sqrt(D)
MIB = 1024 * 1024


def routed(shard, rows, target):
    pairs = []
    for row in range(rows):
        for place in range(RING):
            to = target(row, place)
            if to is not None and to[0] < rows:
                pairs.append((row * RING + place, to[0] * RING + to[1]))
    return lax.ppermute(shard, "tm", pairs)


def mix(tiles, position):
    return (tiles.astype(jnp.float32) + position).astype(jnp.bfloat16)


def times(left, right):
    return jnp.dot(left, right, preferred_element_type=jnp.float32)


def against(queries, pairs):
    keys = jnp.concatenate([pairs[:, :D], pairs[:, D:]], axis=0)
    return lax.dot_general(queries, keys, (((1,), (1,)), ((), ())), preferred_element_type=jnp.float32)


def spread(mixed):
    lane = lax.broadcasted_iota(jnp.int32, mixed.shape, 1)
    zero = jnp.zeros_like(mixed)
    rows = jnp.concatenate([jnp.where(lane < MD, mixed, zero), jnp.where(lane < MD, zero, mixed)], axis=0)
    return jnp.concatenate([rows, jnp.ones_like(rows)], axis=1)


def absent(frame, offsets):
    column = lax.broadcasted_iota(jnp.int32, (1, 2 * len(offsets) * PAIRS), 1)
    part = (column // PAIRS) % len(offsets)
    bias = jnp.zeros(column.shape, jnp.float32)
    for at, offset in enumerate(offsets):
        bias = jnp.where((part == at) & (frame < offset), LOW, bias)
    return bias


def packed_with(both, top):
    values = both[:, :LANES]
    values = values + pltpu.roll(values, MD, 1)
    lane = lax.broadcasted_iota(jnp.int32, values.shape, 1)
    return jnp.where(lane < MD, values, jnp.where(lane < MD + PAIRS, top, both[:, LANES:]))


def ask_kernel(listed, asks):
    shape = asks.shape
    dest = lax.broadcasted_iota(jnp.int32, shape, 0)
    lane = lax.broadcasted_iota(jnp.int32, shape, 1)
    total = jnp.zeros(shape, jnp.int32)
    for run in range(KF // RUN):
        owner = listed[run * RUN] // TILES
        for slot in range(RUN):
            hit = (dest == owner) & (lane == slot)
            total = jnp.where(hit, listed[run * RUN + slot] % TILES, total)
    asks[...] = total


def weights_kernel(w_k, w_v, tpos, *rest):
    w_key, w_value, tpos_pair = rest[-3:]
    zero = jnp.zeros((MD, D), jnp.bfloat16)
    w_key[:MD, :] = jnp.concatenate([w_k[...], zero], axis=1)
    w_key[MD:, :] = jnp.concatenate([zero, w_k[...]], axis=1)
    for part in range(4):
        w_value[part * MD : (part + 1) * MD, :] = w_v[...]
    tpos_pair[...] = jnp.concatenate([tpos[...], tpos[...]], axis=1)


def pick_kernel(asked, own, *rest):
    outgoing = rest[-1]

    def one(dest, carry):
        for slot in range(RUN):
            outgoing[dest * RUN + slot] = own[asked[dest, slot]]
        return carry

    lax.fori_loop(0, asked.shape[0], one, 0)


def keyed_kernel(place, listed, q, incoming, b1, c1, a, tpos, w_key, packed, tiles, mixed):
    frame = place[0]
    y = frame % RING
    step = pl.program_id(0)
    count = q.shape[0]
    rows = count * TT
    part_rows = 2 * PAIRS
    bias = absent(frame, EARLY)
    several = range(SHARED)
    for k in several:
        c = step * SHARED + k
        for s in range(KSEL):
            run = 2 * s + c // RUN
            tiles[k, s] = incoming[(listed[run * RUN] // TILES) * RUN + c % RUN]
        mixed[k, :, 0] = mix(jnp.where(y == 0, c1[:, k], b1[:, k]), tpos[0:1, :])
        mixed[k, :, 1] = mix(a[:, k], tpos[3:4, :])
    keyed = mix(tiles[...], tpos[6:7, :]).reshape(SHARED, KSEL * PAIRS, LANES)
    near = mixed[...].reshape(SHARED, count * part_rows, LANES)
    keyed_pairs = [times(keyed[k], w_key[...]).astype(jnp.bfloat16) for k in several]
    near_pairs = [times(near[k], w_key[...]).astype(jnp.bfloat16) for k in several]
    part = lambda x, t: x[t * part_rows : (t + 1) * part_rows]
    scores = [against(q[:, k].reshape(rows, D), keyed_pairs[k]) for k in several]
    near_scores = [
        jnp.concatenate([against(q[t, k], part(near_pairs[k], t)) for t in range(count)], axis=0) + bias
        for k in several
    ]
    tops = [
        jnp.maximum(
            jnp.max(scores[k], axis=-1, keepdims=True), jnp.max(near_scores[k], axis=-1, keepdims=True)
        )
        for k in several
    ]
    weights = [jnp.exp2((scores[k] - tops[k]) * EXP2_SCALE).astype(jnp.bfloat16) for k in several]
    near_weights = [jnp.exp2((near_scores[k] - tops[k]) * EXP2_SCALE).astype(jnp.bfloat16) for k in several]
    both = [times(weights[k], spread(keyed[k])) for k in several]
    both = [
        both[k]
        + jnp.concatenate(
            [times(near_weights[k][t * TT : (t + 1) * TT], spread(part(near[k], t))) for t in range(count)],
            axis=0,
        )
        for k in several
    ]
    for k in several:
        packed[:, k] = packed_with(both[k], tops[k]).reshape(count, TT, LANES)


def final_kernel(
    place, q, r2, r3, c1, d2, r6, packed, tpos, w_key, w_value, w_o, cot, branch, grad, mixed
):
    frame = place[0]
    y = frame % RING
    step = pl.program_id(0)
    mixed[:, 0] = mix(r2[...], tpos[1:2, :])
    mixed[:, 1] = mix(r3[...], tpos[2:3, :])
    mixed[:, 2] = mix(jnp.where(y == 0, d2[...], c1[...]), tpos[4:5, :])
    mixed[:, 3] = mix(r6[...], tpos[5:6, :])
    part_rows = 4 * PAIRS
    flat = mixed[...].reshape(BLOCK * part_rows, LANES)
    pairs = times(flat, w_key[...]).astype(jnp.bfloat16)
    tiles = range(BLOCK)
    part = lambda x, t: x[t * part_rows : (t + 1) * part_rows]
    scores = jnp.concatenate([against(q[t], part(pairs, t)) for t in tiles], axis=0)
    scores = scores + absent(frame, LATE)
    earlier = packed[...].reshape(BLOCK * TT, LANES)
    earlier_top = earlier[:, MD : MD + 1]
    top = jnp.maximum(jnp.max(scores, axis=-1, keepdims=True), earlier_top)
    weights = jnp.exp2((scores - top) * EXP2_SCALE).astype(jnp.bfloat16)
    both = jnp.concatenate(
        [times(weights[t * TT : (t + 1) * TT], spread(part(flat, t))) for t in tiles], axis=0
    )
    scaled = earlier * jnp.exp2((earlier_top - top) * EXP2_SCALE)
    lane = lax.broadcasted_iota(jnp.int32, earlier.shape, 1)
    summed = both[:, :LANES] + jnp.where(lane < MD, scaled, 0.0)
    summed = summed / (both[:, LANES:] + scaled[:, MD + PAIRS : MD + PAIRS + 1])
    high = summed.astype(jnp.bfloat16)
    low = (summed - high.astype(jnp.float32)).astype(jnp.bfloat16)
    attended = times(jnp.concatenate([high, low], axis=1), w_value[...]).astype(jnp.bfloat16)
    branch[...] = times(attended, w_o[...]).astype(jnp.bfloat16).reshape(branch.shape)
    term = lax.dot_general(
        attended, cot[...].reshape(BLOCK * TT, D), (((0,), (0,)), ((), ())), preferred_element_type=jnp.float32
    )

    @pl.when(step == 0)
    def _():
        grad[...] = term

    @pl.when(step > 0)
    def _():
        grad[...] += term


def per_device(queries, memory, tpos, w_k, w_v, w_o, keyframes, cot):
    place = lax.axis_index("tm")[None]
    devices = lax.axis_size("tm")
    rows = devices // RING
    groups = TILES // CLASSES
    own = memory[0, 0].reshape(TILES, PAIRS, LANES)
    listed = keyframes.reshape(KF)
    in_smem = pl.BlockSpec(memory_space=pltpu.SMEM)
    in_vmem = pl.BlockSpec(memory_space=pltpu.VMEM)

    asks = pl.pallas_call(
        ask_kernel,
        out_shape=jax.ShapeDtypeStruct((devices, LANES), jnp.int32),
        in_specs=[in_smem],
        out_specs=in_vmem,
        name="ask",
    )(listed)
    own, asks = lax.optimization_barrier((own, asks))
    a = routed(own, rows, lambda z, y: (z + 1, y))
    b1 = routed(own, rows, lambda z, y: (z, y + 1) if y < 3 else None)
    y = place[0] % RING
    c1 = routed(a, rows, lambda z, y: (z, (y + 1) % RING))
    r2 = routed(jnp.where(y > 1, a, own), rows, lambda z, y: (z, (y + 2) % RING))
    r3 = routed(jnp.where(y == 0, own, a), rows, lambda z, y: (z, (y - 1) % RING))
    asked = lax.all_to_all(asks, "tm", split_axis=0, concat_axis=0, tiled=True)
    w_key, w_value, tpos_pair = pl.pallas_call(
        weights_kernel,
        out_shape=[
            jax.ShapeDtypeStruct((LANES, 2 * D), jnp.bfloat16),
            jax.ShapeDtypeStruct((2 * LANES, D), jnp.bfloat16),
            jax.ShapeDtypeStruct((7, LANES), jnp.float32),
        ],
        in_specs=[in_vmem] * 3 + [pl.BlockSpec(memory_space=pl.ANY)] * 2,
        out_specs=[in_vmem] * 3,
        name="weights",
    )(w_k, w_v, tpos, a, b1)
    outgoing = pl.pallas_call(
        pick_kernel,
        out_shape=jax.ShapeDtypeStruct((devices * RUN, PAIRS, LANES), jnp.bfloat16),
        in_specs=[in_smem, in_vmem] + [pl.BlockSpec(memory_space=pl.ANY)] * 1,
        out_specs=in_vmem,
        compiler_params=pltpu.CompilerParams(vmem_limit_bytes=56 * MIB),
        name="pick",
    )(asked, own, w_key)
    incoming = lax.all_to_all(outgoing, "tm", split_axis=0, concat_axis=0, tiled=True)
    r6 = routed(r2, rows, lambda z, y: (z + 1, y))
    d2 = routed(c1, rows, lambda z, y: (z + 1, y) if y == 0 else None)
    q_tiles = queries[0, 0].reshape(TILES, TT, D)
    whole = lambda *shape: pl.BlockSpec(shape, lambda i, *_: (0,) * len(shape))
    tile_block = pl.BlockSpec((BLOCK, PAIRS, LANES), lambda i, *_: (i, 0, 0))
    row_block = lambda width: pl.BlockSpec((BLOCK, TT, width), lambda i, *_: (i, 0, 0))
    by_class = lambda x: x.reshape((groups, CLASSES) + x.shape[1:])
    class_block = lambda *tile: pl.BlockSpec((groups, SHARED) + tile, lambda i, *_: (0, i) + (0,) * len(tile))
    packed = pl.pallas_call(
        keyed_kernel,
        grid_spec=pltpu.PrefetchScalarGridSpec(
            num_scalar_prefetch=2,
            grid=(CLASSES // SHARED,),
            in_specs=[class_block(TT, D), whole(devices * RUN, PAIRS, LANES)]
            + [class_block(PAIRS, LANES)] * 3
            + [whole(7, LANES), whole(LANES, 2 * D)],
            out_specs=class_block(TT, LANES),
            scratch_shapes=[
                pltpu.VMEM((SHARED, KSEL, PAIRS, LANES), jnp.bfloat16),
                pltpu.VMEM((SHARED, groups, 2, PAIRS, LANES), jnp.bfloat16),
            ],
        ),
        out_shape=jax.ShapeDtypeStruct((groups, CLASSES, TT, LANES), jnp.float32),
        compiler_params=pltpu.CompilerParams(vmem_limit_bytes=56 * MIB),
        name="keyed",
    )(
        place,
        listed,
        by_class(q_tiles),
        incoming,
        by_class(b1),
        by_class(c1),
        by_class(a),
        tpos_pair,
        w_key,
    )
    branch, grad = pl.pallas_call(
        final_kernel,
        grid_spec=pltpu.PrefetchScalarGridSpec(
            num_scalar_prefetch=1,
            grid=(TILES // BLOCK,),
            in_specs=[row_block(D)]
            + [tile_block] * 5
            + [
                row_block(LANES),
                whole(7, LANES),
                whole(LANES, 2 * D),
                whole(2 * LANES, D),
                whole(D, D),
                row_block(D),
            ],
            out_specs=[row_block(D), whole(D, D)],
            scratch_shapes=[pltpu.VMEM((BLOCK, 4, PAIRS, LANES), jnp.bfloat16)],
        ),
        out_shape=[
            jax.ShapeDtypeStruct((TILES, TT, D), jnp.bfloat16),
            jax.ShapeDtypeStruct((D, D), jnp.float32),
        ],
        compiler_params=pltpu.CompilerParams(vmem_limit_bytes=56 * MIB),
        name="final",
    )(
        place,
        q_tiles,
        r2,
        r3,
        c1,
        d2,
        r6,
        packed.reshape(TILES, TT, LANES),
        tpos_pair,
        w_key,
        w_value,
        w_o,
        cot[0, 0].reshape(TILES, TT, D),
    )

    parts = lax.all_to_all(
        grad.reshape(devices, D // devices, D), "tm", split_axis=0, concat_axis=0, tiled=True
    )
    videos = lax.axis_size("video")
    summed = jnp.sum(parts, axis=0) * (1.0 / math.sqrt(videos * devices * TILES * TT))
    step = 1
    while step < videos:
        summed = summed + lax.ppermute(summed, "video", [(i, i ^ step) for i in range(videos)])
        step *= 2
    return branch.reshape(queries.shape), summed


def solution(mesh):
    in_specs = (
        P("video", "tm", None, None),
        P("video", "tm", None, None),
        P(),
        P(),
        P(),
        P(),
        P("video", "tm", None),
        P("video", "tm", None, None),
    )
    out_specs = (P("video", "tm", None, None), P("tm", None))
    return jax.shard_map(
        per_device, mesh=mesh, in_specs=in_specs, out_specs=out_specs, check_vma=False
    )
```

```python
import math

import jax
import jax.numpy as jnp
from jax import lax
from jax.experimental import pallas as pl
from jax.experimental.pallas import tpu as pltpu
from jax.sharding import PartitionSpec as P

D = 256
MD = 64
TT = 64
TILES = 64
KF = 64
KSEL = 8
CLASSES = 8
RUN = 4
RING = 4
PAIRS = TT // 2
LANES = 2 * MD
BLOCK = 16
EARLY = (1, 4)
LATE = (2, 3, 5, 6)
SHARED = 4
LOW = -1e30
EXP2_SCALE = math.log2(math.e) / math.sqrt(D)
MIB = 1024 * 1024


def routed(shard, rows, target):
    pairs = []
    for row in range(rows):
        for place in range(RING):
            to = target(row, place)
            if to is not None and to[0] < rows:
                pairs.append((row * RING + place, to[0] * RING + to[1]))
    return lax.ppermute(shard, "tm", pairs)


def mix(tiles, position):
    return (tiles.astype(jnp.float32) + position).astype(jnp.bfloat16)


def times(left, right):
    return jnp.dot(left, right, preferred_element_type=jnp.float32)


def against(queries, pairs):
    keys = jnp.concatenate([pairs[:, :D], pairs[:, D:]], axis=0)
    return lax.dot_general(queries, keys, (((1,), (1,)), ((), ())), preferred_element_type=jnp.float32)


def spread(mixed):
    lane = lax.broadcasted_iota(jnp.int32, mixed.shape, 1)
    zero = jnp.zeros_like(mixed)
    rows = jnp.concatenate([jnp.where(lane < MD, mixed, zero), jnp.where(lane < MD, zero, mixed)], axis=0)
    return jnp.concatenate([rows, jnp.ones_like(rows)], axis=1)


def absent(frame, offsets):
    column = lax.broadcasted_iota(jnp.int32, (1, 2 * len(offsets) * PAIRS), 1)
    part = (column // PAIRS) % len(offsets)
    bias = jnp.zeros(column.shape, jnp.float32)
    for at, offset in enumerate(offsets):
        bias = jnp.where((part == at) & (frame < offset), LOW, bias)
    return bias


def packed_with(both, top):
    values = both[:, :LANES]
    values = values + pltpu.roll(values, MD, 1)
    lane = lax.broadcasted_iota(jnp.int32, values.shape, 1)
    return jnp.where(lane < MD, values, jnp.where(lane < MD + PAIRS, top, both[:, LANES:]))


def ask_kernel(listed, asks):
    shape = asks.shape
    dest = lax.broadcasted_iota(jnp.int32, shape, 0)
    lane = lax.broadcasted_iota(jnp.int32, shape, 1)
    total = jnp.zeros(shape, jnp.int32)
    for run in range(KF // RUN):
        owner = listed[run * RUN] // TILES
        for slot in range(RUN):
            hit = (dest == owner) & (lane == slot)
            total = jnp.where(hit, listed[run * RUN + slot] % TILES, total)
    asks[...] = total


def weights_kernel(w_k, w_v, tpos, *rest):
    w_key, w_value, tpos_pair = rest[-3:]
    zero = jnp.zeros((MD, D), jnp.bfloat16)
    w_key[:MD, :] = jnp.concatenate([w_k[...], zero], axis=1)
    w_key[MD:, :] = jnp.concatenate([zero, w_k[...]], axis=1)
    for part in range(4):
        w_value[part * MD : (part + 1) * MD, :] = w_v[...]
    tpos_pair[...] = jnp.concatenate([tpos[...], tpos[...]], axis=1)


def pick_kernel(asked, own, *rest):
    outgoing = rest[-1]

    def one(dest, carry):
        for slot in range(RUN):
            outgoing[dest * RUN + slot] = own[asked[dest, slot]]
        return carry

    lax.fori_loop(0, asked.shape[0], one, 0)


def keyed_kernel(place, listed, q, incoming, b1, c1, a, tpos, w_key, packed, tiles, mixed):
    frame = place[0]
    y = frame % RING
    step = pl.program_id(0)
    count = q.shape[0]
    rows = count * TT
    part_rows = 2 * PAIRS
    bias = absent(frame, EARLY)
    several = range(SHARED)
    for k in several:
        c = step * SHARED + k
        for s in range(KSEL):
            run = 2 * s + c // RUN
            tiles[k, s] = incoming[(listed[run * RUN] // TILES) * RUN + c % RUN]
        mixed[k, :, 0] = mix(jnp.where(y == 0, c1[:, k], b1[:, k]), tpos[0:1, :])
        mixed[k, :, 1] = mix(a[:, k], tpos[3:4, :])
    keyed = mix(tiles[...], tpos[6:7, :]).reshape(SHARED, KSEL * PAIRS, LANES)
    near = mixed[...].reshape(SHARED, count * part_rows, LANES)
    keyed_pairs = [times(keyed[k], w_key[...]).astype(jnp.bfloat16) for k in several]
    near_pairs = [times(near[k], w_key[...]).astype(jnp.bfloat16) for k in several]
    part = lambda x, t: x[t * part_rows : (t + 1) * part_rows]
    scores = [against(q[:, k].reshape(rows, D), keyed_pairs[k]) for k in several]
    near_scores = [
        jnp.concatenate([against(q[t, k], part(near_pairs[k], t)) for t in range(count)], axis=0) + bias
        for k in several
    ]
    tops = [
        jnp.maximum(
            jnp.max(scores[k], axis=-1, keepdims=True), jnp.max(near_scores[k], axis=-1, keepdims=True)
        )
        for k in several
    ]
    weights = [jnp.exp2((scores[k] - tops[k]) * EXP2_SCALE).astype(jnp.bfloat16) for k in several]
    near_weights = [jnp.exp2((near_scores[k] - tops[k]) * EXP2_SCALE).astype(jnp.bfloat16) for k in several]
    both = [times(weights[k], spread(keyed[k])) for k in several]
    both = [
        both[k]
        + jnp.concatenate(
            [times(near_weights[k][t * TT : (t + 1) * TT], spread(part(near[k], t))) for t in range(count)],
            axis=0,
        )
        for k in several
    ]
    for k in several:
        packed[:, k] = packed_with(both[k], tops[k]).reshape(count, TT, LANES)


def final_kernel(
    place, q, r2, r3, c1, d2, r6, packed, tpos, w_key, w_value, w_o, cot, branch, grad, mixed
):
    frame = place[0]
    y = frame % RING
    step = pl.program_id(0)
    mixed[:, 0] = mix(r2[...], tpos[1:2, :])
    mixed[:, 1] = mix(r3[...], tpos[2:3, :])
    mixed[:, 2] = mix(jnp.where(y == 0, d2[...], c1[...]), tpos[4:5, :])
    mixed[:, 3] = mix(r6[...], tpos[5:6, :])
    part_rows = 4 * PAIRS
    flat = mixed[...].reshape(BLOCK * part_rows, LANES)
    pairs = times(flat, w_key[...]).astype(jnp.bfloat16)
    tiles = range(BLOCK)
    part = lambda x, t: x[t * part_rows : (t + 1) * part_rows]
    scores = jnp.concatenate([against(q[t], part(pairs, t)) for t in tiles], axis=0)
    scores = scores + absent(frame, LATE)
    earlier = packed[...].reshape(BLOCK * TT, LANES)
    earlier_top = earlier[:, MD : MD + 1]
    top = jnp.maximum(jnp.max(scores, axis=-1, keepdims=True), earlier_top)
    weights = jnp.exp2((scores - top) * EXP2_SCALE).astype(jnp.bfloat16)
    both = jnp.concatenate(
        [times(weights[t * TT : (t + 1) * TT], spread(part(flat, t))) for t in tiles], axis=0
    )
    scaled = earlier * jnp.exp2((earlier_top - top) * EXP2_SCALE)
    lane = lax.broadcasted_iota(jnp.int32, earlier.shape, 1)
    summed = both[:, :LANES] + jnp.where(lane < MD, scaled, 0.0)
    summed = summed / (both[:, LANES:] + scaled[:, MD + PAIRS : MD + PAIRS + 1])
    high = summed.astype(jnp.bfloat16)
    low = (summed - high.astype(jnp.float32)).astype(jnp.bfloat16)
    attended = times(jnp.concatenate([high, low], axis=1), w_value[...]).astype(jnp.bfloat16)
    branch[...] = times(attended, w_o[...]).astype(jnp.bfloat16).reshape(branch.shape)
    term = lax.dot_general(
        attended, cot[...].reshape(BLOCK * TT, D), (((0,), (0,)), ((), ())), preferred_element_type=jnp.float32
    )

    @pl.when(step == 0)
    def _():
        grad[...] = term

    @pl.when(step > 0)
    def _():
        grad[...] += term


def per_device(queries, memory, tpos, w_k, w_v, w_o, keyframes, cot):
    place = lax.axis_index("tm")[None]
    devices = lax.axis_size("tm")
    rows = devices // RING
    groups = TILES // CLASSES
    own = memory[0, 0].reshape(TILES, PAIRS, LANES)
    listed = keyframes.reshape(KF)
    in_smem = pl.BlockSpec(memory_space=pltpu.SMEM)
    in_vmem = pl.BlockSpec(memory_space=pltpu.VMEM)

    asks = pl.pallas_call(
        ask_kernel,
        out_shape=jax.ShapeDtypeStruct((devices, LANES), jnp.int32),
        in_specs=[in_smem],
        out_specs=in_vmem,
        name="ask",
    )(listed)
    own, asks = lax.optimization_barrier((own, asks))
    a = routed(own, rows, lambda z, y: (z + 1, y))
    b1 = routed(own, rows, lambda z, y: (z, y + 1) if y < 3 else None)
    y = place[0] % RING
    c1 = routed(a, rows, lambda z, y: (z, (y + 1) % RING))
    x2 = jnp.where(y > 1, a, own)
    r2 = routed(x2, rows, lambda z, y: (z, (y + 2) % RING))
    x3 = jnp.where(y == 0, own, a)
    r3 = routed(x3, rows, lambda z, y: (z, (y - 1) % RING))
    asked = lax.all_to_all(asks, "tm", split_axis=0, concat_axis=0, tiled=True)
    w_key, w_value, tpos_pair = pl.pallas_call(
        weights_kernel,
        out_shape=[
            jax.ShapeDtypeStruct((LANES, 2 * D), jnp.bfloat16),
            jax.ShapeDtypeStruct((2 * LANES, D), jnp.bfloat16),
            jax.ShapeDtypeStruct((7, LANES), jnp.float32),
        ],
        in_specs=[in_vmem] * 3 + [pl.BlockSpec(memory_space=pl.ANY)] * 0,
        out_specs=[in_vmem] * 3,
        name="weights",
    )(w_k, w_v, tpos)
    outgoing = pl.pallas_call(
        pick_kernel,
        out_shape=jax.ShapeDtypeStruct((devices * RUN, PAIRS, LANES), jnp.bfloat16),
        in_specs=[in_smem, in_vmem] + [pl.BlockSpec(memory_space=pl.ANY)] * 2,
        out_specs=in_vmem,
        compiler_params=pltpu.CompilerParams(vmem_limit_bytes=60 * MIB),
        name="pick",
    )(asked, own, x2, b1)
    incoming = lax.all_to_all(outgoing, "tm", split_axis=0, concat_axis=0, tiled=True)
    r6 = routed(r2, rows, lambda z, y: (z + 1, y))
    d2 = routed(c1, rows, lambda z, y: (z + 1, y) if y == 0 else None)
    q_tiles = queries[0, 0].reshape(TILES, TT, D)
    whole = lambda *shape: pl.BlockSpec(shape, lambda i, *_: (0,) * len(shape))
    tile_block = pl.BlockSpec((BLOCK, PAIRS, LANES), lambda i, *_: (i, 0, 0))
    row_block = lambda width: pl.BlockSpec((BLOCK, TT, width), lambda i, *_: (i, 0, 0))
    by_class = lambda x: x.reshape((groups, CLASSES) + x.shape[1:])
    class_block = lambda *tile: pl.BlockSpec((groups, SHARED) + tile, lambda i, *_: (0, i) + (0,) * len(tile))
    packed = pl.pallas_call(
        keyed_kernel,
        grid_spec=pltpu.PrefetchScalarGridSpec(
            num_scalar_prefetch=2,
            grid=(CLASSES // SHARED,),
            in_specs=[class_block(TT, D), whole(devices * RUN, PAIRS, LANES)]
            + [class_block(PAIRS, LANES)] * 3
            + [whole(7, LANES), whole(LANES, 2 * D)],
            out_specs=class_block(TT, LANES),
            scratch_shapes=[
                pltpu.VMEM((SHARED, KSEL, PAIRS, LANES), jnp.bfloat16),
                pltpu.VMEM((SHARED, groups, 2, PAIRS, LANES), jnp.bfloat16),
            ],
        ),
        out_shape=jax.ShapeDtypeStruct((groups, CLASSES, TT, LANES), jnp.float32),
        compiler_params=pltpu.CompilerParams(vmem_limit_bytes=60 * MIB),
        name="keyed",
    )(
        place,
        listed,
        by_class(q_tiles),
        incoming,
        by_class(b1),
        by_class(c1),
        by_class(a),
        tpos_pair,
        w_key,
    )
    branch, grad = pl.pallas_call(
        final_kernel,
        grid_spec=pltpu.PrefetchScalarGridSpec(
            num_scalar_prefetch=1,
            grid=(TILES // BLOCK,),
            in_specs=[row_block(D)]
            + [tile_block] * 5
            + [
                row_block(LANES),
                whole(7, LANES),
                whole(LANES, 2 * D),
                whole(2 * LANES, D),
                whole(D, D),
                row_block(D),
            ],
            out_specs=[row_block(D), whole(D, D)],
            scratch_shapes=[pltpu.VMEM((BLOCK, 4, PAIRS, LANES), jnp.bfloat16)],
        ),
        out_shape=[
            jax.ShapeDtypeStruct((TILES, TT, D), jnp.bfloat16),
            jax.ShapeDtypeStruct((D, D), jnp.float32),
        ],
        compiler_params=pltpu.CompilerParams(vmem_limit_bytes=60 * MIB),
        name="final",
    )(
        place,
        q_tiles,
        r2,
        r3,
        c1,
        d2,
        r6,
        packed.reshape(TILES, TT, LANES),
        tpos_pair,
        w_key,
        w_value,
        w_o,
        cot[0, 0].reshape(TILES, TT, D),
    )

    parts = lax.all_to_all(
        grad.reshape(devices, D // devices, D), "tm", split_axis=0, concat_axis=0, tiled=True
    )
    videos = lax.axis_size("video")
    summed = jnp.sum(parts, axis=0) * (1.0 / math.sqrt(videos * devices * TILES * TT))
    summed = summed + lax.ppermute(summed, "video", [(i, i ^ 1) for i in range(videos)])
    others = [
        lax.ppermute(summed, "video", [(i, (i + chip) % videos) for i in range(videos)])
        for chip in range(2, videos, 2)
    ]
    summed = (summed + others[1]) + (others[0] + others[2])
    return branch.reshape(queries.shape), summed


def solution(mesh):
    in_specs = (
        P("video", "tm", None, None),
        P("video", "tm", None, None),
        P(),
        P(),
        P(),
        P(),
        P("video", "tm", None),
        P("video", "tm", None, None),
    )
    out_specs = (P("video", "tm", None, None), P("tm", None))
    return jax.shard_map(
        per_device, mesh=mesh, in_specs=in_specs, out_specs=out_specs, check_vma=False
    )
```

```python
import math

import jax
import jax.numpy as jnp
from jax import lax
from jax.experimental import pallas as pl
from jax.experimental.pallas import tpu as pltpu
from jax.sharding import PartitionSpec as P

D = 256
MD = 64
TT = 64
TILES = 64
KF = 64
KSEL = 8
CLASSES = 8
RUN = 4
RING = 4
PAIRS = TT // 2
LANES = 2 * MD
BLOCK = 16
EARLY = (1, 4)
LATE = (2, 3, 5, 6)
SHARED = 4
LOW = -1e30
EXP2_SCALE = math.log2(math.e) / math.sqrt(D)
MIB = 1024 * 1024


def routed(shard, rows, target):
    pairs = []
    for row in range(rows):
        for place in range(RING):
            to = target(row, place)
            if to is not None and to[0] < rows:
                pairs.append((row * RING + place, to[0] * RING + to[1]))
    return lax.ppermute(shard, "tm", pairs)


def mix(tiles, position):
    return (tiles.astype(jnp.float32) + position).astype(jnp.bfloat16)


def times(left, right):
    return jnp.dot(left, right, preferred_element_type=jnp.float32)


def against(queries, pairs):
    keys = jnp.concatenate([pairs[:, :D], pairs[:, D:]], axis=0)
    return lax.dot_general(queries, keys, (((1,), (1,)), ((), ())), preferred_element_type=jnp.float32)


def spread(mixed):
    lane = lax.broadcasted_iota(jnp.int32, mixed.shape, 1)
    zero = jnp.zeros_like(mixed)
    rows = jnp.concatenate([jnp.where(lane < MD, mixed, zero), jnp.where(lane < MD, zero, mixed)], axis=0)
    return jnp.concatenate([rows, jnp.ones_like(rows)], axis=1)


def absent(frame, offsets):
    column = lax.broadcasted_iota(jnp.int32, (1, 2 * len(offsets) * PAIRS), 1)
    part = (column // PAIRS) % len(offsets)
    bias = jnp.zeros(column.shape, jnp.float32)
    for at, offset in enumerate(offsets):
        bias = jnp.where((part == at) & (frame < offset), LOW, bias)
    return bias


def packed_with(both, top):
    values = both[:, :LANES]
    values = values + pltpu.roll(values, MD, 1)
    lane = lax.broadcasted_iota(jnp.int32, values.shape, 1)
    return jnp.where(lane < MD, values, jnp.where(lane < MD + PAIRS, top, both[:, LANES:]))


def ask_kernel(listed, asks):
    shape = asks.shape
    dest = lax.broadcasted_iota(jnp.int32, shape, 0)
    lane = lax.broadcasted_iota(jnp.int32, shape, 1)
    total = jnp.zeros(shape, jnp.int32)
    for run in range(KF // RUN):
        owner = listed[run * RUN] // TILES
        for slot in range(RUN):
            hit = (dest == owner) & (lane == slot)
            total = jnp.where(hit, listed[run * RUN + slot] % TILES, total)
    asks[...] = total


def weights_kernel(w_k, w_v, tpos, *rest):
    w_key, w_value, tpos_pair = rest[-3:]
    zero = jnp.zeros((MD, D), jnp.bfloat16)
    w_key[:MD, :] = jnp.concatenate([w_k[...], zero], axis=1)
    w_key[MD:, :] = jnp.concatenate([zero, w_k[...]], axis=1)
    for part in range(4):
        w_value[part * MD : (part + 1) * MD, :] = w_v[...]
    tpos_pair[...] = jnp.concatenate([tpos[...], tpos[...]], axis=1)


def pick_kernel(asked, own, *rest):
    outgoing = rest[-1]

    def one(dest, carry):
        for slot in range(RUN):
            outgoing[dest * RUN + slot] = own[asked[dest, slot]]
        return carry

    lax.fori_loop(0, asked.shape[0], one, 0)


def keyed_kernel(place, listed, q, incoming, b1, c1, a, tpos, w_key, packed, tiles, mixed):
    frame = place[0]
    y = frame % RING
    step = pl.program_id(0)
    count = q.shape[0]
    rows = count * TT
    part_rows = 2 * PAIRS
    bias = absent(frame, EARLY)
    several = range(SHARED)
    for k in several:
        c = step * SHARED + k
        for s in range(KSEL):
            run = 2 * s + c // RUN
            tiles[k, s] = incoming[(listed[run * RUN] // TILES) * RUN + c % RUN]
        mixed[k, :, 0] = mix(jnp.where(y == 0, c1[:, k], b1[:, k]), tpos[0:1, :])
        mixed[k, :, 1] = mix(a[:, k], tpos[3:4, :])
    keyed = mix(tiles[...], tpos[6:7, :]).reshape(SHARED, KSEL * PAIRS, LANES)
    near = mixed[...].reshape(SHARED, count * part_rows, LANES)
    keyed_pairs = [times(keyed[k], w_key[...]).astype(jnp.bfloat16) for k in several]
    near_pairs = [times(near[k], w_key[...]).astype(jnp.bfloat16) for k in several]
    part = lambda x, t: x[t * part_rows : (t + 1) * part_rows]
    scores = [against(q[:, k].reshape(rows, D), keyed_pairs[k]) for k in several]
    near_scores = [
        jnp.concatenate([against(q[t, k], part(near_pairs[k], t)) for t in range(count)], axis=0) + bias
        for k in several
    ]
    tops = [
        jnp.maximum(
            jnp.max(scores[k], axis=-1, keepdims=True), jnp.max(near_scores[k], axis=-1, keepdims=True)
        )
        for k in several
    ]
    weights = [jnp.exp2((scores[k] - tops[k]) * EXP2_SCALE).astype(jnp.bfloat16) for k in several]
    near_weights = [jnp.exp2((near_scores[k] - tops[k]) * EXP2_SCALE).astype(jnp.bfloat16) for k in several]
    both = [times(weights[k], spread(keyed[k])) for k in several]
    both = [
        both[k]
        + jnp.concatenate(
            [times(near_weights[k][t * TT : (t + 1) * TT], spread(part(near[k], t))) for t in range(count)],
            axis=0,
        )
        for k in several
    ]
    for k in several:
        packed[:, k] = packed_with(both[k], tops[k]).reshape(count, TT, LANES)


def final_kernel(
    place, q, r2, r3, c1, d2, r6, packed, tpos, w_key, w_value, w_o, cot, branch, grad, mixed, total
):
    frame = place[0]
    y = frame % RING
    step = pl.program_id(0)
    mixed[:, 0] = mix(r2[...], tpos[1:2, :])
    mixed[:, 1] = mix(r3[...], tpos[2:3, :])
    mixed[:, 2] = mix(jnp.where(y == 0, d2[...], c1[...]), tpos[4:5, :])
    mixed[:, 3] = mix(r6[...], tpos[5:6, :])
    part_rows = 4 * PAIRS
    flat = mixed[...].reshape(BLOCK * part_rows, LANES)
    pairs = times(flat, w_key[...]).astype(jnp.bfloat16)
    tiles = range(BLOCK)
    part = lambda x, t: x[t * part_rows : (t + 1) * part_rows]
    scores = jnp.concatenate([against(q[t], part(pairs, t)) for t in tiles], axis=0)
    scores = scores + absent(frame, LATE)
    earlier = packed[...].reshape(BLOCK * TT, LANES)
    earlier_top = earlier[:, MD : MD + 1]
    top = jnp.maximum(jnp.max(scores, axis=-1, keepdims=True), earlier_top)
    weights = jnp.exp2((scores - top) * EXP2_SCALE).astype(jnp.bfloat16)
    both = jnp.concatenate(
        [times(weights[t * TT : (t + 1) * TT], spread(part(flat, t))) for t in tiles], axis=0
    )
    scaled = earlier * jnp.exp2((earlier_top - top) * EXP2_SCALE)
    lane = lax.broadcasted_iota(jnp.int32, earlier.shape, 1)
    summed = both[:, :LANES] + jnp.where(lane < MD, scaled, 0.0)
    summed = summed / (both[:, LANES:] + scaled[:, MD + PAIRS : MD + PAIRS + 1])
    high = summed.astype(jnp.bfloat16)
    low = (summed - high.astype(jnp.float32)).astype(jnp.bfloat16)
    attended = times(jnp.concatenate([high, low], axis=1), w_value[...]).astype(jnp.bfloat16)
    branch[...] = times(attended, w_o[...]).astype(jnp.bfloat16).reshape(branch.shape)
    term = lax.dot_general(
        attended, cot[...].reshape(BLOCK * TT, D), (((0,), (0,)), ((), ())), preferred_element_type=jnp.float32
    )

    @pl.when(step == 0)
    def _():
        total[...] = term

    @pl.when(step > 0)
    def _():
        total[...] += term

    @pl.when(step == pl.num_programs(0) - 1)
    def _():
        grad[...] = total[...].astype(jnp.bfloat16)


def per_device(queries, memory, tpos, w_k, w_v, w_o, keyframes, cot):
    place = lax.axis_index("tm")[None]
    devices = lax.axis_size("tm")
    rows = devices // RING
    groups = TILES // CLASSES
    own = memory[0, 0].reshape(TILES, PAIRS, LANES)
    listed = keyframes.reshape(KF)
    in_smem = pl.BlockSpec(memory_space=pltpu.SMEM)
    in_vmem = pl.BlockSpec(memory_space=pltpu.VMEM)

    asks = pl.pallas_call(
        ask_kernel,
        out_shape=jax.ShapeDtypeStruct((devices, LANES), jnp.int32),
        in_specs=[in_smem],
        out_specs=in_vmem,
        name="ask",
    )(listed)
    own, asks = lax.optimization_barrier((own, asks))
    a = routed(own, rows, lambda z, y: (z + 1, y))
    b1 = routed(own, rows, lambda z, y: (z, y + 1) if y < 3 else None)
    y = place[0] % RING
    c1 = routed(a, rows, lambda z, y: (z, (y + 1) % RING))
    x2 = jnp.where(y > 1, a, own)
    r2 = routed(x2, rows, lambda z, y: (z, (y + 2) % RING))
    x3 = jnp.where(y == 0, own, a)
    r3 = routed(x3, rows, lambda z, y: (z, (y - 1) % RING))
    asked = lax.all_to_all(asks, "tm", split_axis=0, concat_axis=0, tiled=True)
    w_key, w_value, tpos_pair = pl.pallas_call(
        weights_kernel,
        out_shape=[
            jax.ShapeDtypeStruct((LANES, 2 * D), jnp.bfloat16),
            jax.ShapeDtypeStruct((2 * LANES, D), jnp.bfloat16),
            jax.ShapeDtypeStruct((7, LANES), jnp.float32),
        ],
        in_specs=[in_vmem] * 3 + [pl.BlockSpec(memory_space=pl.ANY)] * 1,
        out_specs=[in_vmem] * 3,
        name="weights",
    )(w_k, w_v, tpos, x2)
    outgoing = pl.pallas_call(
        pick_kernel,
        out_shape=jax.ShapeDtypeStruct((devices * RUN, PAIRS, LANES), jnp.bfloat16),
        in_specs=[in_smem, in_vmem] + [pl.BlockSpec(memory_space=pl.ANY)] * 2,
        out_specs=in_vmem,
        compiler_params=pltpu.CompilerParams(vmem_limit_bytes=60 * MIB),
        name="pick",
    )(asked, own, w_key, b1)
    incoming = lax.all_to_all(outgoing, "tm", split_axis=0, concat_axis=0, tiled=True)
    r6 = routed(r2, rows, lambda z, y: (z + 1, y))
    d2 = routed(c1, rows, lambda z, y: (z + 1, y) if y == 0 else None)
    q_tiles = queries[0, 0].reshape(TILES, TT, D)
    whole = lambda *shape: pl.BlockSpec(shape, lambda i, *_: (0,) * len(shape))
    tile_block = pl.BlockSpec((BLOCK, PAIRS, LANES), lambda i, *_: (i, 0, 0))
    row_block = lambda width: pl.BlockSpec((BLOCK, TT, width), lambda i, *_: (i, 0, 0))
    by_class = lambda x: x.reshape((groups, CLASSES) + x.shape[1:])
    class_block = lambda *tile: pl.BlockSpec((groups, SHARED) + tile, lambda i, *_: (0, i) + (0,) * len(tile))
    packed = pl.pallas_call(
        keyed_kernel,
        grid_spec=pltpu.PrefetchScalarGridSpec(
            num_scalar_prefetch=2,
            grid=(CLASSES // SHARED,),
            in_specs=[class_block(TT, D), whole(devices * RUN, PAIRS, LANES)]
            + [class_block(PAIRS, LANES)] * 3
            + [whole(7, LANES), whole(LANES, 2 * D)],
            out_specs=class_block(TT, LANES),
            scratch_shapes=[
                pltpu.VMEM((SHARED, KSEL, PAIRS, LANES), jnp.bfloat16),
                pltpu.VMEM((SHARED, groups, 2, PAIRS, LANES), jnp.bfloat16),
            ],
        ),
        out_shape=jax.ShapeDtypeStruct((groups, CLASSES, TT, LANES), jnp.float32),
        compiler_params=pltpu.CompilerParams(vmem_limit_bytes=30 * MIB),
        name="keyed",
    )(
        place,
        listed,
        by_class(q_tiles),
        incoming,
        by_class(b1),
        by_class(c1),
        by_class(a),
        tpos_pair,
        w_key,
    )
    branch, grad = pl.pallas_call(
        final_kernel,
        grid_spec=pltpu.PrefetchScalarGridSpec(
            num_scalar_prefetch=1,
            grid=(TILES // BLOCK,),
            in_specs=[row_block(D)]
            + [tile_block] * 5
            + [
                row_block(LANES),
                whole(7, LANES),
                whole(LANES, 2 * D),
                whole(2 * LANES, D),
                whole(D, D),
                row_block(D),
            ],
            out_specs=[row_block(D), whole(D, D)],
            scratch_shapes=[
                pltpu.VMEM((BLOCK, 4, PAIRS, LANES), jnp.bfloat16),
                pltpu.VMEM((D, D), jnp.float32),
            ],
        ),
        out_shape=[
            jax.ShapeDtypeStruct((TILES, TT, D), jnp.bfloat16),
            jax.ShapeDtypeStruct((D, D), jnp.bfloat16),
        ],
        compiler_params=pltpu.CompilerParams(vmem_limit_bytes=30 * MIB),
        name="final",
    )(
        place,
        q_tiles,
        r2,
        r3,
        c1,
        d2,
        r6,
        packed.reshape(TILES, TT, LANES),
        tpos_pair,
        w_key,
        w_value,
        w_o,
        cot[0, 0].reshape(TILES, TT, D),
    )

    parts = lax.all_to_all(
        grad.reshape(devices, D // devices, D), "tm", split_axis=0, concat_axis=0, tiled=True
    )
    videos = lax.axis_size("video")
    summed = jnp.sum(parts.astype(jnp.float32), axis=0) * (1.0 / math.sqrt(videos * devices * TILES * TT))
    summed = summed + lax.ppermute(summed, "video", [(i, i ^ 1) for i in range(videos)])
    others = [
        lax.ppermute(summed, "video", [(i, (i + chip) % videos) for i in range(videos)])
        for chip in range(2, videos, 2)
    ]
    summed = (summed + others[1]) + (others[0] + others[2])
    return branch.reshape(queries.shape), summed


def solution(mesh):
    in_specs = (
        P("video", "tm", None, None),
        P("video", "tm", None, None),
        P(),
        P(),
        P(),
        P(),
        P("video", "tm", None),
        P("video", "tm", None, None),
    )
    out_specs = (P("video", "tm", None, None), P("tm", None))
    return jax.shard_map(
        per_device, mesh=mesh, in_specs=in_specs, out_specs=out_specs, check_vma=False
    )
```

```python
import math

import jax
import jax.numpy as jnp
from jax import lax
from jax.experimental import pallas as pl
from jax.experimental.pallas import tpu as pltpu
from jax.sharding import PartitionSpec as P

D = 256
MD = 64
TT = 64
TILES = 64
KF = 64
KSEL = 8
CLASSES = 8
RUN = 4
RING = 4
PAIRS = TT // 2
LANES = 2 * MD
BLOCK = 16
EARLY = (1, 4)
LATE = (2, 3, 5, 6)
SHARED = 4
LOW = -1e30
EXP2_SCALE = math.log2(math.e) / math.sqrt(D)
MIB = 1024 * 1024


def routed(shard, rows, target):
    pairs = []
    for row in range(rows):
        for place in range(RING):
            to = target(row, place)
            if to is not None and to[0] < rows:
                pairs.append((row * RING + place, to[0] * RING + to[1]))
    return lax.ppermute(shard, "tm", pairs)


def mix(tiles, position):
    return (tiles.astype(jnp.float32) + position).astype(jnp.bfloat16)


def times(left, right):
    return jnp.dot(left, right, preferred_element_type=jnp.float32)


def against(queries, pairs):
    keys = jnp.concatenate([pairs[:, :D], pairs[:, D:]], axis=0)
    return lax.dot_general(queries, keys, (((1,), (1,)), ((), ())), preferred_element_type=jnp.float32)


def spread(mixed):
    lane = lax.broadcasted_iota(jnp.int32, mixed.shape, 1)
    zero = jnp.zeros_like(mixed)
    rows = jnp.concatenate([jnp.where(lane < MD, mixed, zero), jnp.where(lane < MD, zero, mixed)], axis=0)
    return jnp.concatenate([rows, jnp.ones_like(rows)], axis=1)


def absent(frame, offsets):
    column = lax.broadcasted_iota(jnp.int32, (1, 2 * len(offsets) * PAIRS), 1)
    part = (column // PAIRS) % len(offsets)
    bias = jnp.zeros(column.shape, jnp.float32)
    for at, offset in enumerate(offsets):
        bias = jnp.where((part == at) & (frame < offset), LOW, bias)
    return bias


def packed_with(both, top):
    values = both[:, :LANES]
    values = values + pltpu.roll(values, MD, 1)
    lane = lax.broadcasted_iota(jnp.int32, values.shape, 1)
    return jnp.where(lane < MD, values, jnp.where(lane < MD + PAIRS, top, both[:, LANES:]))


def ask_kernel(listed, asks):
    shape = asks.shape
    dest = lax.broadcasted_iota(jnp.int32, shape, 0)
    lane = lax.broadcasted_iota(jnp.int32, shape, 1)
    total = jnp.zeros(shape, jnp.int32)
    for run in range(KF // RUN):
        owner = listed[run * RUN] // TILES
        for slot in range(RUN):
            hit = (dest == owner) & (lane == slot)
            total = jnp.where(hit, listed[run * RUN + slot] % TILES, total)
    asks[...] = total


def weights_kernel(w_k, w_v, tpos, *rest):
    w_key, w_value, tpos_pair = rest[-3:]
    zero = jnp.zeros((MD, D), jnp.bfloat16)
    w_key[:MD, :] = jnp.concatenate([w_k[...], zero], axis=1)
    w_key[MD:, :] = jnp.concatenate([zero, w_k[...]], axis=1)
    for part in range(4):
        w_value[part * MD : (part + 1) * MD, :] = w_v[...]
    tpos_pair[...] = jnp.concatenate([tpos[...], tpos[...]], axis=1)


def pick_kernel(asked, own, *rest):
    outgoing = rest[-1]

    def one(dest, carry):
        for slot in range(RUN):
            outgoing[dest * RUN + slot] = own[asked[dest, slot]]
        return carry

    lax.fori_loop(0, asked.shape[0], one, 0)


def keyed_kernel(place, listed, q, incoming, b1, c1, a, tpos, w_key, packed, tiles, mixed):
    frame = place[0]
    y = frame % RING
    step = pl.program_id(0)
    count = q.shape[0]
    rows = count * TT
    part_rows = 2 * PAIRS
    bias = absent(frame, EARLY)
    several = range(SHARED)
    for k in several:
        c = step * SHARED + k
        for s in range(KSEL):
            run = 2 * s + c // RUN
            tiles[k, s] = incoming[(listed[run * RUN] // TILES) * RUN + c % RUN]
        mixed[k, :, 0] = mix(jnp.where(y == 0, c1[:, k], b1[:, k]), tpos[0:1, :])
        mixed[k, :, 1] = mix(a[:, k], tpos[3:4, :])
    keyed = mix(tiles[...], tpos[6:7, :]).reshape(SHARED, KSEL * PAIRS, LANES)
    near = mixed[...].reshape(SHARED, count * part_rows, LANES)
    keyed_pairs = [times(keyed[k], w_key[...]).astype(jnp.bfloat16) for k in several]
    near_pairs = [times(near[k], w_key[...]).astype(jnp.bfloat16) for k in several]
    part = lambda x, t: x[t * part_rows : (t + 1) * part_rows]
    scores = [against(q[:, k].reshape(rows, D), keyed_pairs[k]) for k in several]
    near_scores = [
        jnp.concatenate([against(q[t, k], part(near_pairs[k], t)) for t in range(count)], axis=0) + bias
        for k in several
    ]
    tops = [
        jnp.maximum(
            jnp.max(scores[k], axis=-1, keepdims=True), jnp.max(near_scores[k], axis=-1, keepdims=True)
        )
        for k in several
    ]
    weights = [jnp.exp2((scores[k] - tops[k]) * EXP2_SCALE).astype(jnp.bfloat16) for k in several]
    near_weights = [jnp.exp2((near_scores[k] - tops[k]) * EXP2_SCALE).astype(jnp.bfloat16) for k in several]
    both = [times(weights[k], spread(keyed[k])) for k in several]
    both = [
        both[k]
        + jnp.concatenate(
            [times(near_weights[k][t * TT : (t + 1) * TT], spread(part(near[k], t))) for t in range(count)],
            axis=0,
        )
        for k in several
    ]
    for k in several:
        packed[:, k] = packed_with(both[k], tops[k]).reshape(count, TT, LANES)


def final_kernel(
    place, q, r2, r3, c1, d2, r6, packed, tpos, w_key, w_value, w_o, cot, branch, grad, mixed, total
):
    frame = place[0]
    y = frame % RING
    step = pl.program_id(0)
    mixed[:, 0] = mix(r2[...], tpos[1:2, :])
    mixed[:, 1] = mix(r3[...], tpos[2:3, :])
    mixed[:, 2] = mix(jnp.where(y == 0, d2[...], c1[...]), tpos[4:5, :])
    mixed[:, 3] = mix(r6[...], tpos[5:6, :])
    part_rows = 4 * PAIRS
    flat = mixed[...].reshape(BLOCK * part_rows, LANES)
    pairs = times(flat, w_key[...]).astype(jnp.bfloat16)
    tiles = range(BLOCK)
    part = lambda x, t: x[t * part_rows : (t + 1) * part_rows]
    scores = jnp.concatenate([against(q[t], part(pairs, t)) for t in tiles], axis=0)
    scores = scores + absent(frame, LATE)
    earlier = packed[...].reshape(BLOCK * TT, LANES)
    earlier_top = earlier[:, MD : MD + 1]
    top = jnp.maximum(jnp.max(scores, axis=-1, keepdims=True), earlier_top)
    weights = jnp.exp2((scores - top) * EXP2_SCALE).astype(jnp.bfloat16)
    both = jnp.concatenate(
        [times(weights[t * TT : (t + 1) * TT], spread(part(flat, t))) for t in tiles], axis=0
    )
    scaled = earlier * jnp.exp2((earlier_top - top) * EXP2_SCALE)
    lane = lax.broadcasted_iota(jnp.int32, earlier.shape, 1)
    summed = both[:, :LANES] + jnp.where(lane < MD, scaled, 0.0)
    summed = summed / (both[:, LANES:] + scaled[:, MD + PAIRS : MD + PAIRS + 1])
    high = summed.astype(jnp.bfloat16)
    low = (summed - high.astype(jnp.float32)).astype(jnp.bfloat16)
    attended = times(jnp.concatenate([high, low], axis=1), w_value[...]).astype(jnp.bfloat16)
    branch[...] = times(attended, w_o[...]).astype(jnp.bfloat16).reshape(branch.shape)
    term = lax.dot_general(
        attended, cot[...].reshape(BLOCK * TT, D), (((0,), (0,)), ((), ())), preferred_element_type=jnp.float32
    )

    @pl.when(step == 0)
    def _():
        total[...] = term

    @pl.when(step > 0)
    def _():
        total[...] += term

    @pl.when(step == pl.num_programs(0) - 1)
    def _():
        grad[...] = total[...].astype(jnp.bfloat16)


def per_device(queries, memory, tpos, w_k, w_v, w_o, keyframes, cot):
    place = lax.axis_index("tm")[None]
    devices = lax.axis_size("tm")
    rows = devices // RING
    groups = TILES // CLASSES
    own = memory[0, 0].reshape(TILES, PAIRS, LANES)
    listed = keyframes.reshape(KF)
    in_smem = pl.BlockSpec(memory_space=pltpu.SMEM)
    in_vmem = pl.BlockSpec(memory_space=pltpu.VMEM)

    asks = pl.pallas_call(
        ask_kernel,
        out_shape=jax.ShapeDtypeStruct((devices, LANES), jnp.int32),
        in_specs=[in_smem],
        out_specs=in_vmem,
        compiler_params=pltpu.CompilerParams(vmem_limit_bytes=8 * MIB),
        name="ask",
    )(listed)
    own, asks = lax.optimization_barrier((own, asks))
    a = routed(own, rows, lambda z, y: (z + 1, y))
    b1 = routed(own, rows, lambda z, y: (z, y + 1) if y < 3 else None)
    y = place[0] % RING
    c1 = routed(a, rows, lambda z, y: (z, (y + 1) % RING))
    x2 = jnp.where(y > 1, a, own)
    r2 = routed(x2, rows, lambda z, y: (z, (y + 2) % RING))
    x3 = jnp.where(y == 0, own, a)
    r3 = routed(x3, rows, lambda z, y: (z, (y - 1) % RING))
    asked = lax.all_to_all(asks, "tm", split_axis=0, concat_axis=0, tiled=True)
    w_key, w_value, tpos_pair = pl.pallas_call(
        weights_kernel,
        out_shape=[
            jax.ShapeDtypeStruct((LANES, 2 * D), jnp.bfloat16),
            jax.ShapeDtypeStruct((2 * LANES, D), jnp.bfloat16),
            jax.ShapeDtypeStruct((7, LANES), jnp.float32),
        ],
        in_specs=[in_vmem] * 3 + [pl.BlockSpec(memory_space=pl.ANY)] * 1,
        out_specs=[in_vmem] * 3,
        compiler_params=pltpu.CompilerParams(vmem_limit_bytes=8 * MIB),
        name="weights",
    )(w_k, w_v, tpos, x2)
    outgoing = pl.pallas_call(
        pick_kernel,
        out_shape=jax.ShapeDtypeStruct((devices * RUN, PAIRS, LANES), jnp.bfloat16),
        in_specs=[in_smem, in_vmem] + [pl.BlockSpec(memory_space=pl.ANY)] * 2,
        out_specs=in_vmem,
        compiler_params=pltpu.CompilerParams(vmem_limit_bytes=8 * MIB),
        name="pick",
    )(asked, own, w_key, b1)
    incoming = lax.all_to_all(outgoing, "tm", split_axis=0, concat_axis=0, tiled=True)
    r6 = routed(r2, rows, lambda z, y: (z + 1, y))
    d2 = routed(c1, rows, lambda z, y: (z + 1, y) if y == 0 else None)
    q_tiles = queries[0, 0].reshape(TILES, TT, D)
    whole = lambda *shape: pl.BlockSpec(shape, lambda i, *_: (0,) * len(shape))
    tile_block = pl.BlockSpec((BLOCK, PAIRS, LANES), lambda i, *_: (i, 0, 0))
    row_block = lambda width: pl.BlockSpec((BLOCK, TT, width), lambda i, *_: (i, 0, 0))
    by_class = lambda x: x.reshape((groups, CLASSES) + x.shape[1:])
    class_block = lambda *tile: pl.BlockSpec((groups, SHARED) + tile, lambda i, *_: (0, i) + (0,) * len(tile))
    packed = pl.pallas_call(
        keyed_kernel,
        grid_spec=pltpu.PrefetchScalarGridSpec(
            num_scalar_prefetch=2,
            grid=(CLASSES // SHARED,),
            in_specs=[class_block(TT, D), whole(devices * RUN, PAIRS, LANES)]
            + [class_block(PAIRS, LANES)] * 3
            + [whole(7, LANES), whole(LANES, 2 * D)],
            out_specs=class_block(TT, LANES),
            scratch_shapes=[
                pltpu.VMEM((SHARED, KSEL, PAIRS, LANES), jnp.bfloat16),
                pltpu.VMEM((SHARED, groups, 2, PAIRS, LANES), jnp.bfloat16),
            ],
        ),
        out_shape=jax.ShapeDtypeStruct((groups, CLASSES, TT, LANES), jnp.float32),
        compiler_params=pltpu.CompilerParams(vmem_limit_bytes=30 * MIB),
        name="keyed",
    )(
        place,
        listed,
        by_class(q_tiles),
        incoming,
        by_class(b1),
        by_class(c1),
        by_class(a),
        tpos_pair,
        w_key,
    )
    branch, grad = pl.pallas_call(
        final_kernel,
        grid_spec=pltpu.PrefetchScalarGridSpec(
            num_scalar_prefetch=1,
            grid=(TILES // BLOCK,),
            in_specs=[row_block(D)]
            + [tile_block] * 5
            + [
                row_block(LANES),
                whole(7, LANES),
                whole(LANES, 2 * D),
                whole(2 * LANES, D),
                whole(D, D),
                row_block(D),
            ],
            out_specs=[row_block(D), whole(D, D)],
            scratch_shapes=[
                pltpu.VMEM((BLOCK, 4, PAIRS, LANES), jnp.bfloat16),
                pltpu.VMEM((D, D), jnp.float32),
            ],
        ),
        out_shape=[
            jax.ShapeDtypeStruct((TILES, TT, D), jnp.bfloat16),
            jax.ShapeDtypeStruct((D, D), jnp.bfloat16),
        ],
        compiler_params=pltpu.CompilerParams(vmem_limit_bytes=30 * MIB),
        name="final",
    )(
        place,
        q_tiles,
        r2,
        r3,
        c1,
        d2,
        r6,
        packed.reshape(TILES, TT, LANES),
        tpos_pair,
        w_key,
        w_value,
        w_o,
        cot[0, 0].reshape(TILES, TT, D),
    )

    parts = lax.all_to_all(
        grad.reshape(devices, D // devices, D), "tm", split_axis=0, concat_axis=0, tiled=True
    )
    videos = lax.axis_size("video")
    summed = jnp.sum(parts.astype(jnp.float32), axis=0) * (1.0 / math.sqrt(videos * devices * TILES * TT))
    summed = summed + lax.ppermute(summed, "video", [(i, i ^ 1) for i in range(videos)])
    others = [
        lax.ppermute(summed, "video", [(i, (i + chip) % videos) for i in range(videos)])
        for chip in range(2, videos, 2)
    ]
    summed = (summed + others[1]) + (others[0] + others[2])
    return branch.reshape(queries.shape), summed


def solution(mesh):
    in_specs = (
        P("video", "tm", None, None),
        P("video", "tm", None, None),
        P(),
        P(),
        P(),
        P(),
        P("video", "tm", None),
        P("video", "tm", None, None),
    )
    out_specs = (P("video", "tm", None, None), P("tm", None))
    return jax.shard_map(
        per_device, mesh=mesh, in_specs=in_specs, out_specs=out_specs, check_vma=False
    )
```

```python
import math

import jax
import jax.numpy as jnp
from jax import lax
from jax.experimental import pallas as pl
from jax.experimental.pallas import tpu as pltpu
from jax.sharding import PartitionSpec as P

D = 256
MD = 64
TT = 64
TILES = 64
KF = 64
KSEL = 8
CLASSES = 8
RUN = 4
RING = 4
PAIRS = TT // 2
LANES = 2 * MD
BLOCK = 16
EARLY = (1, 4)
LATE = (2, 3, 5, 6)
SHARED = 4
LOW = -1e30
EXP2_SCALE = math.log2(math.e) / math.sqrt(D)
MIB = 1024 * 1024


def routed(shard, rows, target):
    pairs = []
    for row in range(rows):
        for place in range(RING):
            to = target(row, place)
            if to is not None and to[0] < rows:
                pairs.append((row * RING + place, to[0] * RING + to[1]))
    return lax.ppermute(shard, "tm", pairs)


def mix(tiles, position):
    return (tiles.astype(jnp.float32) + position).astype(jnp.bfloat16)


def times(left, right):
    return jnp.dot(left, right, preferred_element_type=jnp.float32)


def against(queries, pairs):
    keys = jnp.concatenate([pairs[:, :D], pairs[:, D:]], axis=0)
    return lax.dot_general(queries, keys, (((1,), (1,)), ((), ())), preferred_element_type=jnp.float32)


def spread(mixed):
    lane = lax.broadcasted_iota(jnp.int32, mixed.shape, 1)
    zero = jnp.zeros_like(mixed)
    rows = jnp.concatenate([jnp.where(lane < MD, mixed, zero), jnp.where(lane < MD, zero, mixed)], axis=0)
    return jnp.concatenate([rows, jnp.ones_like(rows)], axis=1)


def absent(frame, offsets):
    column = lax.broadcasted_iota(jnp.int32, (1, 2 * len(offsets) * PAIRS), 1)
    part = (column // PAIRS) % len(offsets)
    bias = jnp.zeros(column.shape, jnp.float32)
    for at, offset in enumerate(offsets):
        bias = jnp.where((part == at) & (frame < offset), LOW, bias)
    return bias


def packed_with(both, top):
    values = both[:, :LANES]
    values = values + pltpu.roll(values, MD, 1)
    lane = lax.broadcasted_iota(jnp.int32, values.shape, 1)
    return jnp.where(lane < MD, values, jnp.where(lane < MD + PAIRS, top, both[:, LANES:]))


def ask_kernel(listed, asks):
    shape = asks.shape
    dest = lax.broadcasted_iota(jnp.int32, shape, 0)
    lane = lax.broadcasted_iota(jnp.int32, shape, 1)
    total = jnp.zeros(shape, jnp.int32)
    for run in range(KF // RUN):
        owner = listed[run * RUN] // TILES
        for slot in range(RUN):
            hit = (dest == owner) & (lane == slot)
            total = jnp.where(hit, listed[run * RUN + slot] % TILES, total)
    asks[...] = total


def weights_kernel(w_k, w_v, tpos, *rest):
    w_key, w_value, tpos_pair = rest[-3:]
    zero = jnp.zeros((MD, D), jnp.bfloat16)
    w_key[:MD, :] = jnp.concatenate([w_k[...], zero], axis=1)
    w_key[MD:, :] = jnp.concatenate([zero, w_k[...]], axis=1)
    for part in range(4):
        w_value[part * MD : (part + 1) * MD, :] = w_v[...]
    tpos_pair[...] = jnp.concatenate([tpos[...], tpos[...]], axis=1)


def pick_kernel(asked, own, *rest):
    outgoing = rest[-1]

    def one(dest, carry):
        for slot in range(RUN):
            outgoing[dest * RUN + slot] = own[asked[dest, slot]]
        return carry

    lax.fori_loop(0, asked.shape[0], one, 0)


def keyed_kernel(place, listed, q, incoming, b1, c1, a, tpos, w_key, packed, tiles, mixed):
    frame = place[0]
    y = frame % RING
    step = pl.program_id(0)
    count = q.shape[0]
    rows = count * TT
    part_rows = 2 * PAIRS
    bias = absent(frame, EARLY)
    several = range(SHARED)
    for k in several:
        c = step * SHARED + k
        for s in range(KSEL):
            run = 2 * s + c // RUN
            tiles[k, s] = incoming[(listed[run * RUN] // TILES) * RUN + c % RUN]
        mixed[k, :, 0] = mix(jnp.where(y == 0, c1[:, k], b1[:, k]), tpos[0:1, :])
        mixed[k, :, 1] = mix(a[:, k], tpos[3:4, :])
    keyed = mix(tiles[...], tpos[6:7, :]).reshape(SHARED, KSEL * PAIRS, LANES)
    near = mixed[...].reshape(SHARED, count * part_rows, LANES)
    keyed_pairs = [times(keyed[k], w_key[...]).astype(jnp.bfloat16) for k in several]
    near_pairs = [times(near[k], w_key[...]).astype(jnp.bfloat16) for k in several]
    part = lambda x, t: x[t * part_rows : (t + 1) * part_rows]
    scores = [against(q[:, k].reshape(rows, D), keyed_pairs[k]) for k in several]
    near_scores = [
        jnp.concatenate([against(q[t, k], part(near_pairs[k], t)) for t in range(count)], axis=0) + bias
        for k in several
    ]
    tops = [
        jnp.maximum(
            jnp.max(scores[k], axis=-1, keepdims=True), jnp.max(near_scores[k], axis=-1, keepdims=True)
        )
        for k in several
    ]
    weights = [jnp.exp2((scores[k] - tops[k]) * EXP2_SCALE).astype(jnp.bfloat16) for k in several]
    near_weights = [jnp.exp2((near_scores[k] - tops[k]) * EXP2_SCALE).astype(jnp.bfloat16) for k in several]
    both = [times(weights[k], spread(keyed[k])) for k in several]
    both = [
        both[k]
        + jnp.concatenate(
            [times(near_weights[k][t * TT : (t + 1) * TT], spread(part(near[k], t))) for t in range(count)],
            axis=0,
        )
        for k in several
    ]
    for k in several:
        packed[:, k] = packed_with(both[k], tops[k]).reshape(count, TT, LANES)


def final_kernel(
    place, q, r2, r3, c1, d2, r6, packed, tpos, w_key, w_value, w_o, cot, branch, grad, mixed, total
):
    frame = place[0]
    y = frame % RING
    step = pl.program_id(0)
    mixed[:, 0] = mix(r2[...], tpos[1:2, :])
    mixed[:, 1] = mix(r3[...], tpos[2:3, :])
    mixed[:, 2] = mix(jnp.where(y == 0, d2[...], c1[...]), tpos[4:5, :])
    mixed[:, 3] = mix(r6[...], tpos[5:6, :])
    part_rows = 4 * PAIRS
    flat = mixed[...].reshape(BLOCK * part_rows, LANES)
    pairs = times(flat, w_key[...]).astype(jnp.bfloat16)
    tiles = range(BLOCK)
    part = lambda x, t: x[t * part_rows : (t + 1) * part_rows]
    scores = jnp.concatenate([against(q[t], part(pairs, t)) for t in tiles], axis=0)
    scores = scores + absent(frame, LATE)
    earlier = packed[...].reshape(BLOCK * TT, LANES)
    earlier_top = earlier[:, MD : MD + 1]
    top = jnp.maximum(jnp.max(scores, axis=-1, keepdims=True), earlier_top)
    weights = jnp.exp2((scores - top) * EXP2_SCALE).astype(jnp.bfloat16)
    both = jnp.concatenate(
        [times(weights[t * TT : (t + 1) * TT], spread(part(flat, t))) for t in tiles], axis=0
    )
    scaled = earlier * jnp.exp2((earlier_top - top) * EXP2_SCALE)
    lane = lax.broadcasted_iota(jnp.int32, earlier.shape, 1)
    summed = both[:, :LANES] + jnp.where(lane < MD, scaled, 0.0)
    summed = summed / (both[:, LANES:] + scaled[:, MD + PAIRS : MD + PAIRS + 1])
    high = summed.astype(jnp.bfloat16)
    low = (summed - high.astype(jnp.float32)).astype(jnp.bfloat16)
    attended = times(jnp.concatenate([high, low], axis=1), w_value[...]).astype(jnp.bfloat16)
    branch[...] = times(attended, w_o[...]).astype(jnp.bfloat16).reshape(branch.shape)
    term = lax.dot_general(
        attended, cot[...].reshape(BLOCK * TT, D), (((0,), (0,)), ((), ())), preferred_element_type=jnp.float32
    )

    @pl.when(step == 0)
    def _():
        total[...] = term

    @pl.when(step > 0)
    def _():
        total[...] += term

    @pl.when(step == pl.num_programs(0) - 1)
    def _():
        grad[...] = total[...].astype(jnp.bfloat16)


def per_device(queries, memory, tpos, w_k, w_v, w_o, keyframes, cot):
    place = lax.axis_index("tm")[None]
    devices = lax.axis_size("tm")
    rows = devices // RING
    groups = TILES // CLASSES
    own = memory[0, 0].reshape(TILES, PAIRS, LANES)
    listed = keyframes.reshape(KF)
    in_smem = pl.BlockSpec(memory_space=pltpu.SMEM)
    in_vmem = pl.BlockSpec(memory_space=pltpu.VMEM)

    asks = pl.pallas_call(
        ask_kernel,
        out_shape=jax.ShapeDtypeStruct((devices, LANES), jnp.int32),
        in_specs=[in_smem],
        out_specs=in_vmem,
        name="ask",
    )(listed)
    own, asks = lax.optimization_barrier((own, asks))
    a = routed(own, rows, lambda z, y: (z + 1, y))
    b1 = routed(own, rows, lambda z, y: (z, y + 1) if y < 3 else None)
    y = place[0] % RING
    c1 = routed(a, rows, lambda z, y: (z, (y + 1) % RING))
    x2 = jnp.where(y > 1, a, own)
    r2 = routed(x2, rows, lambda z, y: (z, (y + 2) % RING))
    x3 = jnp.where(y == 0, own, a)
    r3 = routed(x3, rows, lambda z, y: (z, (y - 1) % RING))
    asked = lax.all_to_all(asks, "tm", split_axis=0, concat_axis=0, tiled=True)
    w_key, w_value, tpos_pair = pl.pallas_call(
        weights_kernel,
        out_shape=[
            jax.ShapeDtypeStruct((LANES, 2 * D), jnp.bfloat16),
            jax.ShapeDtypeStruct((2 * LANES, D), jnp.bfloat16),
            jax.ShapeDtypeStruct((7, LANES), jnp.float32),
        ],
        in_specs=[in_vmem] * 3 + [pl.BlockSpec(memory_space=pl.ANY)] * 1,
        out_specs=[in_vmem] * 3,
        compiler_params=pltpu.CompilerParams(vmem_limit_bytes=8 * MIB),
        name="weights",
    )(w_k, w_v, tpos, x2)
    outgoing = pl.pallas_call(
        pick_kernel,
        out_shape=jax.ShapeDtypeStruct((devices * RUN, PAIRS, LANES), jnp.bfloat16),
        in_specs=[in_smem, in_vmem] + [pl.BlockSpec(memory_space=pl.ANY)] * 2,
        out_specs=in_vmem,
        compiler_params=pltpu.CompilerParams(vmem_limit_bytes=8 * MIB),
        name="pick",
    )(asked, own, w_key, b1)
    incoming = lax.all_to_all(outgoing, "tm", split_axis=0, concat_axis=0, tiled=True)
    r6 = routed(r2, rows, lambda z, y: (z + 1, y))
    d2 = routed(c1, rows, lambda z, y: (z + 1, y) if y == 0 else None)
    q_tiles = queries[0, 0].reshape(TILES, TT, D)
    whole = lambda *shape: pl.BlockSpec(shape, lambda i, *_: (0,) * len(shape))
    tile_block = pl.BlockSpec((BLOCK, PAIRS, LANES), lambda i, *_: (i, 0, 0))
    row_block = lambda width: pl.BlockSpec((BLOCK, TT, width), lambda i, *_: (i, 0, 0))
    by_class = lambda x: x.reshape((groups, CLASSES) + x.shape[1:])
    class_block = lambda *tile: pl.BlockSpec((groups, SHARED) + tile, lambda i, *_: (0, i) + (0,) * len(tile))
    packed = pl.pallas_call(
        keyed_kernel,
        grid_spec=pltpu.PrefetchScalarGridSpec(
            num_scalar_prefetch=2,
            grid=(CLASSES // SHARED,),
            in_specs=[class_block(TT, D), whole(devices * RUN, PAIRS, LANES)]
            + [class_block(PAIRS, LANES)] * 3
            + [whole(7, LANES), whole(LANES, 2 * D)],
            out_specs=class_block(TT, LANES),
            scratch_shapes=[
                pltpu.VMEM((SHARED, KSEL, PAIRS, LANES), jnp.bfloat16),
                pltpu.VMEM((SHARED, groups, 2, PAIRS, LANES), jnp.bfloat16),
            ],
        ),
        out_shape=jax.ShapeDtypeStruct((groups, CLASSES, TT, LANES), jnp.float32),
        compiler_params=pltpu.CompilerParams(vmem_limit_bytes=30 * MIB),
        name="keyed",
    )(
        place,
        listed,
        by_class(q_tiles),
        incoming,
        by_class(b1),
        by_class(c1),
        by_class(a),
        tpos_pair,
        w_key,
    )
    branch, grad = pl.pallas_call(
        final_kernel,
        grid_spec=pltpu.PrefetchScalarGridSpec(
            num_scalar_prefetch=1,
            grid=(TILES // BLOCK,),
            in_specs=[row_block(D)]
            + [tile_block] * 5
            + [
                row_block(LANES),
                whole(7, LANES),
                whole(LANES, 2 * D),
                whole(2 * LANES, D),
                whole(D, D),
                row_block(D),
            ],
            out_specs=[row_block(D), whole(D, D)],
            scratch_shapes=[
                pltpu.VMEM((BLOCK, 4, PAIRS, LANES), jnp.bfloat16),
                pltpu.VMEM((D, D), jnp.float32),
            ],
        ),
        out_shape=[
            jax.ShapeDtypeStruct((TILES, TT, D), jnp.bfloat16),
            jax.ShapeDtypeStruct((D, D), jnp.bfloat16),
        ],
        compiler_params=pltpu.CompilerParams(vmem_limit_bytes=30 * MIB),
        name="final",
    )(
        place,
        q_tiles,
        r2,
        r3,
        c1,
        d2,
        r6,
        packed.reshape(TILES, TT, LANES),
        tpos_pair,
        w_key,
        w_value,
        w_o,
        cot[0, 0].reshape(TILES, TT, D),
    )

    parts = lax.all_to_all(
        grad.reshape(devices, D // devices, D), "tm", split_axis=0, concat_axis=0, tiled=True
    )
    videos = lax.axis_size("video")
    summed = jnp.sum(parts.astype(jnp.float32), axis=0) * (1.0 / math.sqrt(videos * devices * TILES * TT))
    summed = summed + lax.ppermute(summed, "video", [(i, i ^ 1) for i in range(videos)])
    others = [
        lax.ppermute(summed, "video", [(i, (i + chip) % videos) for i in range(videos)])
        for chip in range(2, videos, 2)
    ]
    summed = (summed + others[1]) + (others[0] + others[2])
    return branch.reshape(queries.shape), summed


def solution(mesh):
    in_specs = (
        P("video", "tm", None, None),
        P("video", "tm", None, None),
        P(),
        P(),
        P(),
        P(),
        P("video", "tm", None),
        P("video", "tm", None, None),
    )
    out_specs = (P("video", "tm", None, None), P("tm", None))
    return jax.shard_map(
        per_device, mesh=mesh, in_specs=in_specs, out_specs=out_specs, check_vma=False
    )
```
